256 devices in a mesh: section: 16 (over z, x_hi), tensor: 8 (over x_lo, y), dp: 2 (over core).
Axes of the slice: x: 4 (x_hi: 2, x_lo: 2; x = x_hi * 2 + x_lo), y: 4, z: 8, core: 2. Of those that a mesh axis runs over, the one named last changes fastest.
Arguments:
- base_weight: bfloat16 [16, 8192, 8192], P('section', ('tensor', 'dp')), may hold values from -0.0625 to 0.0625
- pol_down: bfloat16 [16, 8192, 128], P('section', ('tensor', 'dp')), may hold values from -0.0625 to 0.0625
- pol_up: bfloat16 [16, 128, 8192], P('section', None, ('tensor', 'dp')), may hold values from -0.5 to 0.5
- old_down: bfloat16 [16, 8192, 128], P('section', ('tensor', 'dp')), may hold values from -0.0625 to 0.0625
- old_up: bfloat16 [16, 128, 8192], P('section', None, ('tensor', 'dp')), may hold values from -0.5 to 0.5
- pol_in: bfloat16 [16, 256, 8192], P('section', 'dp', 'tensor'), may hold values from -6 to 6
- ref_in: bfloat16 [16, 256, 8192], P('section', 'dp', 'tensor'), may hold values from -6 to 6
- grad_in: bfloat16 [16, 256, 8192], P('section', 'dp', 'tensor'), may hold values from -6 to 6
- stash: bfloat16 [16, 2, 256, 8192], P('section', None, 'dp', 'tensor'), may hold values from -6 to 6
- fresh_pol: bfloat16 [1, 256, 8192], P(None, 'dp', 'tensor'), may hold values from -6 to 6
- fresh_ref: bfloat16 [1, 256, 8192], P(None, 'dp', 'tensor'), may hold values from -6 to 6
- targets: bfloat16 [2, 256, 8192], P(None, 'dp', 'tensor'), may hold values from -1 to 1
- final_gain: float32 [8192], P('tensor'), may hold values from 0.5 to 1.5
- token_side: int32 [2, 256], P(None, 'dp'), may hold values from 0 to 2, as said below
- ref_logratio: float32 [2, 2], P(None, 'dp'), may hold values from -32 to 32
Outputs:
- pol_out: bfloat16 [16, 256, 8192], P('section', 'dp', 'tensor')
- ref_out: bfloat16 [16, 256, 8192], P('section', 'dp', 'tensor')
- grad_out: bfloat16 [16, 256, 8192], P('section', 'dp', 'tensor')
- grad_down: float32 [16, 8192, 128], P('section', ('tensor', 'dp'))
- grad_up: float32 [16, 128, 8192], P('section', None, ('tensor', 'dp'))
The draws below stay inside these ranges and needn't reach their ends.
Inputs may be any that keep to these rules, and one draw needn't show every extreme that they name: `token_side`: 0 marks padding, 1 a token of the chosen answer, 2 a token of the rejected answer; within the rows of a pair the 1s are a leading run of the first half of its 128 rows and the 2s a leading run of the second half, each run of even length from 2 to half of 128, and one of the two runs fills its half.
All inputs are finite; a program needn't handle non-finite values.
Results may differ from the reference program's by a relative error of at most 0.01.
Values may be sent and summed in bfloat16 or wider, within the bound.
A program may use at most 128 MiB of HBM per device.

```python
import jax
import jax.numpy as jnp
from jax import lax

D = 8192
RANK = 128
TOK = 128
TICKS = 2
LAYERS = 16
PAIRS = 2
TOKENS = 256


def layer_draw(key, layer, profile_power):
    layer_key = jax.random.fold_in(key, layer)
    normal_key = jax.random.fold_in(layer_key, 0)
    phase_key = jax.random.fold_in(layer_key, 2)
    normal_part = jax.random.truncated_normal(normal_key, -6.0, 6.0, (TOKENS, D), jnp.float32)
    phase = jax.random.uniform(phase_key, (), jnp.float32)
    position = jnp.arange(D, dtype=jnp.float32) / D + phase
    profile = jnp.exp2(profile_power * (2.0 * (position - jnp.floor(position)) - 1.0))
    return profile[None, :] * normal_part


def draw_pol_in(key, part):
    profile_power = 0.0
    layers = [layer_draw(key, layer, profile_power) for layer in range(LAYERS)]
    return jnp.stack(layers).astype(jnp.bfloat16)


def draw_targets(key, part):
    profile_power = 0.0
    sources = jnp.stack([layer_draw(key, max(LAYERS - 1 - tick, 0), profile_power) for tick in range(TICKS)])
    key = jax.random.fold_in(key, 11)
    normal_noise = jax.random.truncated_normal(key, -4.0, 4.0, (TICKS, TOKENS, D), jnp.float32)
    noise = normal_noise
    parity = 1.0 - 2.0 * (jnp.arange(TOKENS, dtype=jnp.int32) % 2).astype(jnp.float32)
    combined = 0.9 * parity[None, :, None] * sources + 0.44 * noise
    return (jnp.clip(combined, -4.0, 4.0) * D ** (-0.5)).astype(jnp.bfloat16)


def draw_token_side(key, part):
    key = jax.random.fold_in(key, 23)
    length_key, full_key = jax.random.split(key)
    half = TOK // 2
    lengths = 2 * jax.random.randint(length_key, (TICKS, PAIRS), 1, half // 2 + 1)
    full_side = jax.random.randint(full_key, (TICKS, PAIRS), 0, 2)
    chosen = jnp.where(full_side == 0, half, lengths)
    rejected = jnp.where(full_side == 1, half, lengths)
    position = jnp.arange(TOK, dtype=jnp.int32)
    first_run = position[None, None, :] < chosen[:, :, None]
    second_run = (position[None, None, :] >= half) & (position[None, None, :] < half + rejected[:, :, None])
    side = jnp.where(first_run, 1, 0)
    side = jnp.where(second_run, 2, side)
    return side.reshape(TICKS, TOKENS).astype(jnp.int32)


def levels(own_key, dims, cuts, low, largest):
    loudness = 1.0
    for dim, blocks in cuts:
        draws = jax.random.uniform(jax.random.fold_in(jax.random.fold_in(own_key, 6), dim), (blocks,), jnp.float32, low / len(cuts), largest / len(cuts))
        loudness = loudness * jnp.repeat(jnp.exp(draws), dims[dim] // blocks).reshape((-1,) + (1,) * (len(dims) - 1 - dim))
    return loudness


def centred(key, shape, scale, reach, cuts=(), held_as=jnp.bfloat16):
    level = levels(key, shape, cuts, -0.22, 0.18) if cuts else 1.0
    values = jax.random.normal(key, shape, jnp.float32) * scale * level
    return jnp.minimum(jnp.maximum(values, -reach), reach).astype(held_as)


def setup_inputs(seed: int = 0) -> dict:
    streams_of = jax.random.split(jax.random.key(seed), 16)
    return {
        "base_weight": centred(streams_of[0], (LAYERS, D, D), D ** -0.5, 0.0625, ((0, 16), (1, 16))),
        "pol_down": centred(streams_of[1], (LAYERS, D, RANK), D ** -0.5, 0.0625, ((0, 16), (1, 16))),
        "pol_up": centred(streams_of[2], (LAYERS, RANK, D), RANK ** -0.5, 0.5, ((0, 16), (2, 16))),
        "old_down": centred(streams_of[3], (LAYERS, D, RANK), D ** -0.5, 0.0625, ((0, 16), (1, 16))),
        "old_up": centred(streams_of[4], (LAYERS, RANK, D), RANK ** -0.5, 0.5, ((0, 16), (2, 16))),
        "pol_in": draw_pol_in(jax.random.fold_in(streams_of[15], 71), 0),
        "ref_in": centred(streams_of[6], (LAYERS, TOKENS, D), 1.0, 6.0, ((0, 16), (1, 2), (2, 8))),
        "grad_in": centred(streams_of[7], (LAYERS, TOKENS, D), 1.0, 6.0, ((0, 16), (1, 2), (2, 8))),
        "stash": centred(streams_of[8], (LAYERS, TICKS, TOKENS, D), 1.0, 6.0, ((0, 16), (2, 2), (3, 8))),
        "fresh_pol": centred(streams_of[9], (TICKS - 1, TOKENS, D), 1.0, 6.0, ((1, 2), (2, 8))),
        "fresh_ref": centred(streams_of[10], (TICKS - 1, TOKENS, D), 1.0, 6.0, ((1, 2), (2, 8))),
        "targets": draw_targets(jax.random.fold_in(streams_of[15], 71), 0),
        "final_gain": jnp.clip(1.0 + 0.1 * jax.random.normal(streams_of[12], (D,), jnp.float32), 0.5, 1.5),
        "token_side": draw_token_side(jax.random.fold_in(streams_of[15], 71), 0),
        "ref_logratio": centred(streams_of[14], (TICKS, PAIRS), 8.0, 32.0, ((1, 2),), jnp.float32),
    }


ADAPTER_SCALE = 0.5
MIX_WEIGHT = 0.6
PREF_BETA = 0.1
LOSS_SCALE = 1024.0
NORM_EPSILON = 1e-06

def layer_forward(layer_activation, weight, down_weight, up_weight):
    frozen_weight = jnp.dot(layer_activation, weight, preferred_element_type=jnp.float32)
    adapter_product = jnp.dot(layer_activation, down_weight, preferred_element_type=jnp.float32).astype(jnp.bfloat16)
    combined_output = layer_activation.astype(jnp.float32) + frozen_weight + ADAPTER_SCALE * jnp.dot(adapter_product, up_weight, preferred_element_type=jnp.float32)
    return combined_output.astype(jnp.bfloat16)

def layer_backward(stored_input, incoming_gradient, weight, down_weight, up_weight):
    adapter_product = jnp.dot(stored_input, down_weight, preferred_element_type=jnp.float32).astype(jnp.bfloat16)
    backward_signal = jnp.dot(incoming_gradient, up_weight.T, preferred_element_type=jnp.float32).astype(jnp.bfloat16)
    combined_output = incoming_gradient.astype(jnp.float32) + jnp.dot(incoming_gradient, weight.T, preferred_element_type=jnp.float32)
    combined_output = combined_output + ADAPTER_SCALE * jnp.dot(backward_signal, down_weight.T, preferred_element_type=jnp.float32)
    down_gradient = ADAPTER_SCALE * jnp.dot(stored_input.T, backward_signal, preferred_element_type=jnp.float32)
    up_gradient = ADAPTER_SCALE * jnp.dot(adapter_product.T, incoming_gradient, preferred_element_type=jnp.float32)
    return (combined_output.astype(jnp.bfloat16), down_gradient, up_gradient)

def head_cotangent(hidden, target, gain, side, ref_ratio):
    hidden_f = hidden.astype(jnp.float32)
    target_f = target.astype(jnp.float32)
    sumsq = lax.optimization_barrier(jnp.sum(hidden_f * hidden_f, axis=-1))
    inner = lax.optimization_barrier(jnp.sum(hidden_f * gain * target_f, axis=-1))
    inv_rms = jax.lax.rsqrt(sumsq / D + NORM_EPSILON)
    score = inner * inv_rms
    sign = (side == 1).astype(jnp.float32) - (side == 2).astype(jnp.float32)
    diff = lax.optimization_barrier(jnp.sum((score * sign).reshape(PAIRS, TOK), axis=1))
    margin = PREF_BETA * (diff - ref_ratio)
    scale_pair = -LOSS_SCALE * PREF_BETA * jax.nn.sigmoid(-margin)
    token_weight = jnp.repeat(scale_pair, TOK) * sign
    incoming_gradient = token_weight[:, None] * (inv_rms[:, None] * gain * target_f - (inner * inv_rms ** 3 / D)[:, None] * hidden_f)
    return incoming_gradient.astype(jnp.bfloat16)

def reference(base_weight, pol_down, pol_up, old_down, old_up, pol_in, ref_in, grad_in, stash, fresh_pol, fresh_ref, targets, final_gain, token_side, ref_logratio):
    sections = base_weight.shape[0]
    ref_down = (MIX_WEIGHT * pol_down.astype(jnp.float32) + (1.0 - MIX_WEIGHT) * old_down.astype(jnp.float32)).astype(jnp.bfloat16)
    ref_up = (MIX_WEIGHT * pol_up.astype(jnp.float32) + (1.0 - MIX_WEIGHT) * old_up.astype(jnp.float32)).astype(jnp.bfloat16)
    pol_acts = [pol_in[layer] for layer in range(sections)]
    ref_acts = [ref_in[layer] for layer in range(sections)]
    cotans = [grad_in[layer] for layer in range(sections)]
    down_sums = [jnp.zeros((D, RANK), jnp.float32) for layer in range(sections)]
    up_sums = [jnp.zeros((RANK, D), jnp.float32) for layer in range(sections)]
    for tick_index in range(TICKS):
        pol_next = [layer_forward(pol_acts[layer], base_weight[layer], pol_down[layer], pol_up[layer]) for layer in range(sections)]
        ref_next = [layer_forward(ref_acts[layer], base_weight[layer], ref_down[layer], ref_up[layer]) for layer in range(sections)]
        head_cot = head_cotangent(pol_next[sections - 1], targets[tick_index], final_gain, token_side[tick_index], ref_logratio[tick_index])
        back_next = []
        for layer in range(sections):
            if layer == sections - 1:
                stored_input, incoming_gradient = (pol_acts[layer], head_cot)
            else:
                stored_input, incoming_gradient = (stash[layer, tick_index], cotans[layer])
            result, down_gradient, up_gradient = layer_backward(stored_input, incoming_gradient, base_weight[layer], pol_down[layer], pol_up[layer])
            back_next.append(result)
            down_sums[layer] = down_sums[layer] + down_gradient
            up_sums[layer] = up_sums[layer] + up_gradient
        if tick_index + 1 < TICKS:
            pol_acts = [fresh_pol[tick_index]] + pol_next[:-1]
            ref_acts = [fresh_ref[tick_index]] + ref_next[:-1]
            cotans = back_next[1:] + [jnp.zeros_like(back_next[0])]
    return (jnp.stack(pol_next), jnp.stack(ref_next), jnp.stack(back_next), jnp.stack(down_sums), jnp.stack(up_sums))
```

```python
import functools

import jax
import jax.numpy as jnp
from jax import lax
from jax.experimental import pallas as pl
from jax.experimental.pallas import tpu as pltpu
from jax.sharding import PartitionSpec as P

BF = jnp.bfloat16
F32 = jnp.float32
MESH = pl.DeviceIdType.MESH

NX, NY = 2, 4
NT = NX * NY
ROUTE_ROWS = 128

ADAPTER_SCALE = 0.5
MIX_WEIGHT = 0.6
PREF_BETA = 0.1
LOSS_SCALE = 1024.0
NORM_EPSILON = 1e-06


def nn(a, b):
    return lax.dot_general(a, b, (((1,), (0,)), ((), ())), preferred_element_type=F32)


def nt(a, b):
    return lax.dot_general(a, b, (((1,), (1,)), ((), ())), preferred_element_type=F32)


def tn(a, b):
    return lax.dot_general(a, b, (((0,), (0,)), ((), ())), preferred_element_type=F32)


def mixed(first, second):
    return (MIX_WEIGHT * first.astype(F32) + (1.0 - MIX_WEIGHT) * second.astype(F32)).astype(BF)


def scratch(tok, cb, rank):
    rows, wide = 2 * tok, 2 * cb
    na = ROUTE_ROWS
    nb = rows - na
    ha, hb = na // 2, nb // 2
    piece = tok // NT
    vm = lambda *shape: pltpu.VMEM(shape, BF)
    vf = lambda *shape: pltpu.VMEM(shape, F32)
    dma = lambda *shape: pltpu.SemaphoreType.DMA(shape)
    table = {
        "wb": vm(NX, NY, wide, cb),
        "xin": vm(4, rows, wide),
        "st": vm(2, tok, wide),
        "sb": vm(2, rows, cb),
        "tg": vm(2, rows, cb),
        "dn": vm(wide, rank),
        "do": vm(wide, rank),
        "dr": vm(wide, rank),
        "ur": vm(rank, cb),
        "ax": vf(2, 8, tok),
        "pb": vm(4, NX, NY, rows, cb),
        "ra1": vm(4, 4, na, cb),
        "ra2": vm(4, 2, ha, cb),
        "ra3": vm(4, 2, na, cb),
        "rb1": vm(4, 2, NX, hb, cb),
        "rb2": vm(4, 2, NX, nb, cb),
        "rb3": vm(4, nb, cb),
        "po": vm(4, rows, cb),
        "gb": vm(2, NX, NY, rows, cb),
        "acc": vf(2, rows, cb),
        "bs": vm(2, rows, cb),
        "br": vm(2, rows, cb),
        "co": vm(2, rows, cb),
        "bps": vm(2, rows, rank),
        "bpr": vm(2, tok, rank),
        "hi": vf(2, 2 * NT, 8, rows),
    }
    for i, parts in enumerate((4, 1, 2, 1)):
        table[f"ls{i}"] = vm(tok, parts * rank)
        table[f"ai{i}"] = vm(NT, piece, parts * rank)
        table[f"ao{i}"] = vm(rows, parts * rank)
    table.update(
        {
            "l_sem": dma(24),
            "e_send": dma(24),
            "e_recv": dma(24),
            "r_send": dma(4, 13),
            "r_recv": dma(4, 13),
            "g_send": dma(2, 13),
            "g_recv": dma(2, 13),
            "a_send": dma(4, 3),
            "a_recv": dma(4, 3),
            "h_send": dma(2),
            "h_recv": dma(2),
            "p_send": dma(3),
            "p_recv": dma(3),
            "m_send": dma(9),
            "m_recv": dma(9),
        }
    )
    return table


def kernel(
    names,
    sections,
    width,
    base_weight,
    pol_down,
    pol_up,
    old_down,
    old_up,
    pol_in,
    ref_in,
    grad_in,
    stash,
    fresh_pol,
    fresh_ref,
    targets,
    final_gain,
    token_side,
    ref_logratio,
    pol_out,
    ref_out,
    grad_out,
    grad_down,
    grad_up,
    *buffers,
):
    b = dict(zip(names, buffers))
    wb, xin, pb, gb = b["wb"], b["xin"], b["pb"], b["gb"]
    rows, wide = xin.shape[1:]
    tok, cb = rows // 2, wide // 2
    rank = pol_up.shape[1]
    na = ROUTE_ROWS
    nb = rows - na
    ha, hb = na // 2, nb // 2
    piece = tok // NT

    s = lax.axis_index("section")
    t = lax.axis_index("tensor")
    c = lax.axis_index("dp")
    x, y = t // NY, t % NY
    ox, oc = 1 - x, 1 - c
    y1, y2, y3 = (y + 1) % NY, (y + 2) % NY, (y + 3) % NY
    is_last = s == sections - 1
    is_first = s == 0
    pair = (s, t, oc)
    over = (s, ox * NY + y, c)
    plus = (s, x * NY + y1, c)
    minus = (s, x * NY + y3, c)

    my_rows = pl.ds(pl.multiple_of(c * tok, tok), tok)
    its_rows = pl.ds(pl.multiple_of(oc * tok, tok), tok)
    my_cols = pl.ds(pl.multiple_of(c * cb, cb), cb)
    its_cols = pl.ds(pl.multiple_of(oc * cb, cb), cb)
    my_deep = my_cols
    a_rows, b_rows = pl.ds(0, na), pl.ds(na, nb)

    def send(src, dst, group, index, device):
        return pltpu.make_async_remote_copy(
            src_ref=src,
            dst_ref=dst,
            send_sem=b[group + "_send"].at[index],
            recv_sem=b[group + "_recv"].at[index],
            device_id=device,
            device_id_type=MESH,
        )

    finals = []

    def start(copy):
        copy.start()
        finals.append(copy)

    def weight_cols(xx, yy, core):
        first = pl.multiple_of((xx * NY + yy) * wide + core * cb, cb)
        return base_weight.at[0, :, pl.ds(first, cb)]

    def chunk_of(j):
        step = jnp.where(j == 0, 2, jnp.where(j == 3, 0, 2 * j - 1))
        return (y + step) % NY

    def weight_local(j, side):
        xx, yy = (ox if side == 0 else x), chunk_of(j)
        return pltpu.make_async_copy(
            weight_cols(xx, yy, c), wb.at[xx, yy, my_deep, :], b["l_sem"].at[2 * j + side]
        )

    def weight_remote(j, side):
        xx, yy = (ox if side == 0 else x), chunk_of(j)
        return send(weight_cols(xx, yy, oc), wb.at[xx, yy, my_deep, :], "e", 2 * j + side, pair)

    own = {
        "dn": (pol_down.at[0], b["dn"].at[my_deep]),
        "do": (old_down.at[0], b["do"].at[my_deep]),
        "p0": (pol_in.at[0], xin.at[0, my_rows]),
        "r0": (ref_in.at[0], xin.at[1, my_rows]),
        "g0": (grad_in.at[0, :, my_cols], gb.at[0, x, y, my_rows]),
        "s0": (stash.at[0, 0, :, my_cols], b["sb"].at[0, my_rows]),
        "s1": (stash.at[0, 1, :, my_cols], b["sb"].at[1, my_rows]),
        "t0": (targets.at[0, :, my_cols], b["tg"].at[0, my_rows]),
        "t1": (targets.at[1, :, my_cols], b["tg"].at[1, my_rows]),
        "st": (stash.at[0], b["st"]),
        "fp": (fresh_pol.at[0], xin.at[2, my_rows]),
        "fr": (fresh_ref.at[0], xin.at[3, my_rows]),
    }
    away = {
        "dn": (pol_down.at[0], b["dn"].at[my_deep]),
        "do": (old_down.at[0], b["do"].at[my_deep]),
        "p0": (pol_in.at[0], xin.at[0, my_rows]),
        "r0": (ref_in.at[0], xin.at[1, my_rows]),
        "g0": (grad_in.at[0, :, its_cols], gb.at[0, x, y, my_rows]),
        "s0": (stash.at[0, 0, :, its_cols], b["sb"].at[0, my_rows]),
        "s1": (stash.at[0, 1, :, its_cols], b["sb"].at[1, my_rows]),
        "t0": (targets.at[0, :, its_cols], b["tg"].at[0, my_rows]),
        "t1": (targets.at[1, :, its_cols], b["tg"].at[1, my_rows]),
        "ax": (b["ax"].at[c], b["ax"].at[c]),
        "fp": (fresh_pol.at[0], xin.at[2, my_rows]),
        "fr": (fresh_ref.at[0], xin.at[3, my_rows]),
    }
    place = {name: 8 + i for i, name in enumerate(["dn", "do", "p0", "r0", "g0", "s0", "s1", "t0", "t1", "st", "fp", "fr", "ax"])}

    def local(name):
        return pltpu.make_async_copy(*own[name], b["l_sem"].at[place[name]])

    def swap(name):
        return send(*away[name], "e", place[name], pair)

    for name in ("dn", "do", "p0", "r0", "st"):
        local(name).start()
    for j in range(4):
        for side in range(2):
            weight_local(j, side).start()
    for name in ("g0", "s0", "s1", "t0", "t1"):
        local(name).start()

    @pl.when(is_first)
    def _():
        local("fp").start()
        local("fr").start()

    me = 2 * t + c
    barrier = pltpu.get_barrier_semaphore()

    def greet(d, _):
        other = (me + d) % (2 * NT)
        pl.semaphore_signal(barrier, inc=1, device_id=(s, other // 2, other % 2), device_id_type=MESH)
        return 0

    after = ((s + 1) % sections, t, c)
    before = ((s + sections - 1) % sections, t, c)
    lax.fori_loop(1, 2 * NT, greet, 0)
    pl.semaphore_signal(barrier, inc=1, device_id=after, device_id_type=MESH)
    pl.semaphore_signal(barrier, inc=1, device_id=before, device_id_type=MESH)
    pl.semaphore_wait(barrier, 2 * NT + 1)

    start(swap("dn"))
    start(swap("do"))
    start(swap("p0"))
    for j in range(4):
        for side in range(2):
            start(weight_remote(j, side))
    start(swap("r0"))

    side = token_side[...]
    signs = (side == 1).astype(F32) - (side == 2).astype(F32)
    ratios = jnp.broadcast_to(ref_logratio[...], (2, tok))
    b["ax"][c] = jnp.concatenate([signs, ratios, signs, ratios], axis=0)
    for name in ("ax", "t0", "g0", "s0", "s1", "t1"):
        start(swap(name))

    @pl.when(is_first)
    def _():
        swap("fp").start()
        swap("fr").start()

    def part_rows(index):
        return pl.ds(pl.multiple_of(index * piece, piece), piece)

    def sum_send(i):
        ls, ai = b[f"ls{i}"], b[f"ai{i}"]

        def one(d, _):
            tt = (t + d) % NT
            send(ls.at[part_rows(tt)], ai.at[t], "a", (i, 0), (s, tt, c)).start()
            return 0

        lax.fori_loop(1, NT, one, 0)
        ai[t] = ls[part_rows(t)]

    def sum_reduce(i):
        ai, ao = b[f"ai{i}"], b[f"ao{i}"]
        seven = ai.at[pl.ds(0, NT - 1)]
        pltpu.make_async_copy(seven, seven, b["a_recv"].at[i, 0]).wait()
        total = ai[0].astype(F32)
        for d in range(1, NT):
            total += ai[d].astype(F32)
        here = pl.ds(pl.multiple_of(c * tok + t * piece, piece), piece)
        ao[here] = total.astype(BF)

        def one(d, _):
            tt = (t + d) % NT
            send(ao.at[here], ao.at[here], "a", (i, 1), (s, tt, c)).start()
            return 0

        lax.fori_loop(1, NT, one, 0)

    def sum_share(i):
        ao = b[f"ao{i}"]
        most = ao.at[pl.ds(0, piece * (NT - 1))]
        pltpu.make_async_copy(most, most, b["a_recv"].at[i, 1]).wait()
        start(send(ao.at[my_rows], ao.at[my_rows], "a", (i, 2), pair))

    def sum_done(i):
        ao = b[f"ao{i}"]
        send(ao.at[my_rows], ao.at[my_rows], "a", (i, 2), pair).wait_recv()

    def sum_sent(i):
        seven = b[f"ai{i}"].at[pl.ds(0, NT - 1)]
        pltpu.make_async_copy(seven, seven, b["a_send"].at[i, 0]).wait()
        most = b[f"ao{i}"].at[pl.ds(0, piece * (NT - 1))]
        pltpu.make_async_copy(most, most, b["a_send"].at[i, 1]).wait()

    def f32(ref, *index):
        return ref[index].astype(F32)

    def a1(p, j):
        return send(pb.at[p, ox, chunk_of(j), a_rows], b["ra1"].at[p, j], "r", (p, j), over)

    def a2(p, up):
        half = pl.ds(0, ha) if up == 0 else pl.ds(ha, ha)
        return send(pb.at[p, x, y2, half], b["ra2"].at[p, up], "r", (p, 4 + up), plus if up == 0 else minus)

    def b1(p, up):
        half = pl.ds(na, hb) if up == 0 else pl.ds(na + hb, hb)
        return send(pb.at[p, :, y2, half], b["rb1"].at[p, up], "r", (p, 6 + up), plus if up == 0 else minus)

    def b2(p, up):
        yy = y1 if up == 0 else y3
        return send(pb.at[p, :, yy, b_rows], b["rb2"].at[p, up], "r", (p, 8 + up), plus if up == 0 else minus)

    def b3(p):
        return send(pb.at[p, ox, y, b_rows], b["rb3"].at[p], "r", (p, 10), over)

    def a3(p, up):
        yy = y1 if up == 0 else y3
        return send(pb.at[p, x, yy, a_rows], b["ra3"].at[p, up], "r", (p, 11 + up), plus if up == 0 else minus)

    def products(p, first):
        def body(j, _):
            yy = chunk_of(j)
            for which in range(2):
                xx = ox if which == 0 else x
                if first:
                    weight_local(j, which).wait()
                    weight_remote(j, which).wait_recv()
                pb[p, xx, yy] = nn(xin[p], wb[xx, yy]).astype(BF)
                if first and which == 0:
                    a1(p, j).start()
            return 0

        lax.fori_loop(0, 4, body, 0)
        if first:
            finals.extend(a1(p, j) for j in range(4))

    def stage1(p, first):
        if not first:
            start(a1(p, 0))
        start(b1(p, 0))
        start(b1(p, 1))
        if not first:
            for j in range(1, 4):
                start(a1(p, j))

    def stage2(p):
        for up in range(2):
            yy = y1 if up == 0 else y3
            half = pl.ds(na, hb) if up == 0 else pl.ds(na + hb, hb)
            b1(p, up).wait_recv()
            for xx in range(NX):
                pb[p, xx, yy, half] = (f32(pb, p, xx, yy, half) + f32(b["rb1"], p, up, xx)).astype(BF)
            start(b2(p, up))

    def stage3(p):
        a1(p, 0).wait_recv()
        pb[p, x, y2, a_rows] = (f32(pb, p, x, y2, a_rows) + f32(b["ra1"], p, 0)).astype(BF)
        start(a2(p, 0))
        start(a2(p, 1))

    def stage4(p):
        b2(p, 0).wait_recv()
        b2(p, 1).wait_recv()
        pb[p, ox, y, b_rows] = (
            f32(pb, p, ox, y, b_rows) + f32(b["rb2"], p, 0, ox) + f32(b["rb2"], p, 1, ox)
        ).astype(BF)
        start(b3(p))

    def stage5(p):
        for up in range(2):
            yy = y1 if up == 0 else y3
            half = pl.ds(0, ha) if up == 0 else pl.ds(ha, ha)
            rest = pl.ds(ha, ha) if up == 0 else pl.ds(0, ha)
            a1(p, 1 + up).wait_recv()
            a2(p, up).wait_recv()
            pb[p, x, yy, half] = (
                f32(pb, p, x, yy, half) + f32(b["ra1"], p, 1 + up, half) + f32(b["ra2"], p, up)
            ).astype(BF)
            pb[p, x, yy, rest] = (f32(pb, p, x, yy, rest) + f32(b["ra1"], p, 1 + up, rest)).astype(BF)
            start(a3(p, up))

    def finish(p, low, up_ref):
        a1(p, 3).wait_recv()
        a3(p, 0).wait_recv()
        a3(p, 1).wait_recv()
        b3(p).wait_recv()
        summed = (
            f32(pb, p, x, y, a_rows)
            + f32(b["ra1"], p, 3)
            + f32(b["ra3"], p, 0)
            + f32(b["ra3"], p, 1),
            f32(pb, p, x, y, b_rows)
            + f32(b["rb2"], p, 0, x)
            + f32(b["rb2"], p, 1, x)
            + f32(b["rb3"], p),
        )
        for part, total in zip((a_rows, b_rows), summed):
            adapted = ADAPTER_SCALE * nn(low[0][part, low[1]], up_ref)
            b["po"][p, part] = (f32(xin, p, part, my_cols) + total + adapted).astype(BF)

    gain = lambda: final_gain[:, my_cols]

    def head_sums(k):
        @pl.when(is_last)
        def _():
            h = f32(b["po"], 2 * k)
            squares = jnp.sum(h * h, axis=1, keepdims=True)
            inner = jnp.sum(h * gain() * f32(b["tg"], k), axis=1, keepdims=True)
            lane = lax.broadcasted_iota(jnp.int32, (rows, 128), 1)
            both = jnp.where(lane == 0, squares, inner).T
            b["hi"][k, me] = both[:8]

            def one(d, _):
                other = (me + d) % (2 * NT)
                slot = b["hi"].at[k, me]
                send(slot, slot, "h", k, (s, other // 2, other % 2)).start()
                return 0

            lax.fori_loop(1, 2 * NT, one, 0)

    def head_cotangent(k):
        @pl.when(is_last)
        def _():
            others = b["hi"].at[k, pl.ds(0, 2 * NT - 1)]
            pltpu.make_async_copy(others, others, b["h_recv"].at[k]).wait()
            total = b["hi"][k, 0]
            for d in range(1, 2 * NT):
                total += b["hi"][k, d]
            sums = jnp.concatenate([total] * 16, axis=0).T
            squares, inner = sums[:, 0:1], sums[:, 1:2]
            rms = lax.rsqrt(squares / width + NORM_EPSILON)
            for p in range(2):
                part = slice(p * tok, (p + 1) * tok)
                aux = jnp.concatenate([b["ax"][p]] * (tok // 8), axis=0).T
                sign, ratio = aux[:, k : k + 1], aux[0:1, 2 + k : 3 + k]
                r, dot = rms[part], inner[part]
                margin = PREF_BETA * (jnp.sum(dot * r * sign, axis=0, keepdims=True) - ratio)
                weight = -LOSS_SCALE * PREF_BETA * jax.nn.sigmoid(-margin) * sign
                h = f32(b["po"], 2 * k, part)
                g = weight * (r * gain() * f32(b["tg"], k, part) - (dot * r * r * r / width) * h)
                gb[k, x, y, part] = g.astype(BF)

            pltpu.make_async_copy(others, others, b["h_send"].at[k]).wait()

    def g_copy(k, i):
        own_x, away_x, full = x, ox, pl.ds(0, rows)
        first, second = pl.ds(0, tok), pl.ds(tok, tok)
        xx, yy, part, device = (
            (own_x, y, full, plus),
            (own_x, y, full, minus),
            (own_x, y, a_rows, over),
            (own_x, y, b_rows, over),
            (away_x, y, a_rows, plus),
            (away_x, y, a_rows, minus),
            (own_x, y3, first, plus),
            (own_x, y1, second, minus),
            (own_x, y3, b_rows, over),
            (own_x, y1, b_rows, over),
            (away_x, y3, pl.ds(0, ha), plus),
            (away_x, y1, pl.ds(ha, ha), minus),
            (own_x, y2, b_rows, over),
        )[i]
        block = gb.at[k, xx, yy, part]
        return send(block, block, "g", (k, i), device)

    def g_start(k, *which):
        for i in which:
            start(g_copy(k, i))

    def g_wait(k, *which):
        for i in which:
            g_copy(k, i).wait_recv()

    def gather1(k):
        g_start(k, 2, 0, 1, 3)

    def gather2(k):
        g_wait(k, 2)
        g_start(k, 4, 5)

    def gather3(k):
        g_wait(k, 0)
        g_start(k, 6, 8)
        g_wait(k, 1)
        g_start(k, 7, 9)

    def gather4(k):
        g_wait(k, 4)
        g_start(k, 10)
        g_wait(k, 5)
        g_start(k, 11)

    def gather5(k):
        g_wait(k, 6, 7)
        g_start(k, 12)

    def through(k, xx, yys, fresh=False):
        def body(j, _):
            yy = (y + j) % NY
            for core in range(2):
                deep = pl.ds(core * cb, cb)
                term = nt(gb[k, xx, yy], wb[xx, yy, deep])
                if fresh:
                    b["acc"][core] = jnp.where(j == yys[0], term, b["acc"][core] + term)
                else:
                    b["acc"][core] += term
            return 0

        lax.fori_loop(yys[0], yys[1], body, 0)

    def products_back(k):
        for core in range(2):
            b["acc"][core] = jnp.zeros((rows, cb), F32)
        through(k, x, (0, NY))
        g_wait(k, 3, 8, 9, 10, 11, 12)
        through(k, ox, (0, NY))
        b["bs"][k] = b["acc"][oc].astype(BF)
        start(send(b["bs"].at[k], b["br"].at[k], "m", k, pair))

    def back_start(k):
        b["bps"][k] = nt(gb[k, x, y], pol_up[0]).astype(BF)
        start(send(b["bps"].at[k, its_rows], b["bpr"].at[k], "m", 2 + k, pair))

    def back_sum(k, i):
        send(b["bps"].at[k, its_rows], b["bpr"].at[k], "m", 2 + k, pair).wait_recv()
        b[f"ls{i}"][...] = (f32(b["bps"], k, my_rows) + f32(b["bpr"], k)).astype(BF)
        sum_send(i)

    def back_finish(k, i):
        send(b["bs"].at[k], b["br"].at[k], "m", k, pair).wait_recv()
        back = b[f"ao{i}"][...]
        adapted = ADAPTER_SCALE * nt(back, b["dn"][my_deep])
        b["co"][k] = (f32(gb, k, x, y) + b["acc"][c] + f32(b["br"], k) + adapted).astype(BF)

    def gradients(k, i):
        back = b[f"ao{i}"][...]
        stored = jnp.where(is_last, xin[2 * k, :, my_cols], b["sb"][k])
        low_pol = b["ao0"][:, 0:rank] if k == 0 else b["ao2"][:, 0:rank]
        low = jnp.where(is_last, low_pol, b["ao0"][:, (2 + k) * rank : (3 + k) * rank])
        down = ADAPTER_SCALE * tn(stored, back)
        up = ADAPTER_SCALE * tn(low, gb[k, x, y])
        if k == 0:
            grad_down[0] = down
            grad_up[0] = up
        else:
            grad_down[0] += down
            grad_up[0] += up

    def pass_copy(i):
        if i < 2:
            return send(b["po"].at[i], xin.at[2 + i, :, my_cols], "p", i, after)
        return send(b["co"].at[0], gb.at[1, x, y], "p", 2, before)

    def pass_on(i):
        @pl.when(is_first if i == 2 else is_last)
        def _():
            pass

        @pl.when(jnp.logical_not(is_first if i == 2 else is_last))
        def _():
            pass_copy(i).start()

    def pass_sent(i):
        @pl.when(jnp.logical_not(is_first if i == 2 else is_last))
        def _():
            pass_copy(i).wait_send()

    def taken(i):
        block = xin.at[2 + i, :, my_cols]
        return send(block, block, "m", 4 + i, pair)

    def take(i):
        @pl.when(jnp.logical_not(is_first))
        def _():
            pass_copy(i).wait_recv()
            taken(i).start()

    def take_done(i):
        name = ("fp", "fr")[i]

        @pl.when(is_first)
        def _():
            local(name).wait()
            swap(name).wait()

        @pl.when(jnp.logical_not(is_first))
        def _():
            taken(i).wait()

    def out_copy(i, src, out):
        return send(src.at[its_rows], out.at[0, :, my_cols], "m", 6 + i, pair)

    def put_out(i, src, out):
        start(out_copy(i, src, out))
        out[0, :, my_cols] = src[my_rows]

    for name in ("dn", "do", "p0", "r0", "st"):
        local(name).wait()
    swap("dn").wait_recv()
    swap("do").wait_recv()
    b["dr"][...] = mixed(b["dn"][...], b["do"][...])
    b["ur"][...] = mixed(pol_up[0], old_up[0])
    for q, (ref, down) in enumerate(
        (
            (xin.at[0, my_rows], b["dn"]),
            (xin.at[1, my_rows], b["dr"]),
            (b["st"].at[0], b["dn"]),
            (b["st"].at[1], b["dn"]),
        )
    ):
        b["ls0"][:, q * rank : (q + 1) * rank] = nn(ref[...], down[...]).astype(BF)
    sum_send(0)
    swap("p0").wait_recv()
    products(0, True)
    stage1(0, True)
    sum_reduce(0)
    stage2(0)
    stage3(0)
    swap("r0").wait_recv()
    products(1, False)
    sum_share(0)
    stage4(0)
    stage1(1, False)
    stage5(0)
    stage2(1)
    sum_done(0)
    finish(0, (b["ao0"], pl.ds(0, rank)), pol_up[0])
    pass_on(0)
    for name in ("g0", "s0", "s1", "t0", "t1"):
        local(name).wait()
        swap(name).wait_recv()
    swap("ax").wait_recv()
    head_sums(0)
    stage3(1)
    stage4(1)
    head_cotangent(0)
    gather1(0)
    back_start(0)
    stage5(1)
    gather2(0)
    back_sum(0, 1)
    finish(1, (b["ao0"], pl.ds(rank, rank)), b["ur"][...])
    pass_on(1)
    gather3(0)
    take(0)
    gather4(0)
    sum_reduce(1)
    take_done(0)
    products(2, False)
    gather5(0)
    stage1(2, False)
    sum_share(1)
    products_back(0)
    take(1)
    stage2(2)
    stage3(2)
    sum_done(1)
    back_finish(0, 1)
    pass_on(2)
    gradients_early = functools.partial(gradients, 0, 1)
    take_done(1)
    for q, down in enumerate((b["dn"], b["dr"])):
        b["ls2"][:, q * rank : (q + 1) * rank] = nn(xin[2 + q, my_rows], down[...]).astype(BF)
    sum_send(2)
    products(3, False)
    stage4(2)
    stage1(3, False)
    sum_reduce(2)
    gradients_early()
    stage5(2)
    stage2(3)
    sum_share(2)
    sum_done(2)
    finish(2, (b["ao2"], pl.ds(0, rank)), pol_up[0])
    head_sums(1)
    put_out(0, b["po"].at[2], pol_out)
    stage3(3)
    stage4(3)
    head_cotangent(1)

    @pl.when(jnp.logical_not(is_last))
    def _():
        pass_copy(2).wait_recv()

    gather1(1)
    back_start(1)
    stage5(3)
    gather2(1)
    back_sum(1, 3)
    finish(3, (b["ao2"], pl.ds(rank, rank)), b["ur"][...])
    put_out(1, b["po"].at[3], ref_out)
    gather3(1)
    gather4(1)
    sum_reduce(3)
    gather5(1)
    sum_share(3)
    sum_done(3)
    gradients(1, 3)
    products_back(1)
    back_finish(1, 3)
    put_out(2, b["co"].at[1], grad_out)

    out_copy(0, b["po"].at[2], pol_out).wait_recv()
    out_copy(1, b["po"].at[3], ref_out).wait_recv()
    out_copy(2, b["co"].at[1], grad_out).wait_recv()
    for copy in finals:
        copy.wait_send()
    for i in range(3):
        pass_sent(i)
    for i in range(4):
        sum_sent(i)


def on_device(sections, width, *operands):
    pol_in = operands[5]
    tok, wide = pol_in.shape[1:]
    cb = wide // 2
    rank = operands[1].shape[2]
    operands = list(operands)
    operands[12] = operands[12].reshape(1, wide)
    table = scratch(tok, cb, rank)
    anywhere = pl.BlockSpec(memory_space=pl.ANY)
    inside = pl.BlockSpec(memory_space=pltpu.VMEM)
    in_vmem = (2, 4, 12, 13, 14)
    outs = (
        jax.ShapeDtypeStruct((1, tok, wide), BF),
        jax.ShapeDtypeStruct((1, tok, wide), BF),
        jax.ShapeDtypeStruct((1, tok, wide), BF),
        jax.ShapeDtypeStruct((1, cb, rank), F32),
        jax.ShapeDtypeStruct((1, rank, cb), F32),
    )
    return pl.pallas_call(
        functools.partial(kernel, tuple(table), sections, width),
        out_shape=outs,
        in_specs=[inside if i in in_vmem else anywhere for i in range(15)],
        out_specs=[inside] * 5,
        scratch_shapes=list(table.values()),
        compiler_params=pltpu.CompilerParams(
            collective_id=0, has_side_effects=True, vmem_limit_bytes=56 * 1024 * 1024
        ),
        name="relay",
    )(*operands)


def solution(mesh):
    in_specs = (
        P("section", ("tensor", "dp"), None),
        P("section", ("tensor", "dp"), None),
        P("section", None, ("tensor", "dp")),
        P("section", ("tensor", "dp"), None),
        P("section", None, ("tensor", "dp")),
        P("section", "dp", "tensor"),
        P("section", "dp", "tensor"),
        P("section", "dp", "tensor"),
        P("section", None, "dp", "tensor"),
        P(None, "dp", "tensor"),
        P(None, "dp", "tensor"),
        P(None, "dp", "tensor"),
        P("tensor"),
        P(None, "dp"),
        P(None, "dp"),
    )
    out_specs = (
        P("section", "dp", "tensor"),
        P("section", "dp", "tensor"),
        P("section", "dp", "tensor"),
        P("section", ("tensor", "dp"), None),
        P("section", None, ("tensor", "dp")),
    )
    sections = mesh.shape["section"]

    def whole(base_weight, *rest):
        body = functools.partial(on_device, sections, base_weight.shape[1])
        return jax.shard_map(
            body, mesh=mesh, in_specs=in_specs, out_specs=out_specs, check_vma=False
        )(base_weight, *rest)

    return whole
```

```python
import functools
from types import SimpleNamespace

import jax
import jax.numpy as jnp
from jax import lax
from jax.experimental import pallas as pl
from jax.experimental.pallas import tpu as pltpu
from jax.sharding import PartitionSpec as P

BF = jnp.bfloat16
F32 = jnp.float32
MESH = pl.DeviceIdType.MESH

NX, NY = 2, 4
NT = NX * NY
HALVES = 2
ROWS_LAST = (((48, 80), (64, 48), (32, 80), (48, 48)), ((96, 96), (64, 112)))
ROWS_OTHERS = (((32, 64), (48, 32), (64, 32), (48, 48)), ((112, 80), (80, 96)))

ADAPTER_SCALE = 0.5
MIX_WEIGHT = 0.6
PREF_BETA = 0.1
LOSS_SCALE = 1024.0
NORM_EPSILON = 1e-06

PR, A1, A2, A3, B1, B2, B3, FIN, ARS, ARR, ARH, ARD,     HS, HW, G, TH, BP, ACC, CFIN, CW, TK, TD, GR, END = range(24)
PLAN_LAST = (
    (PR, 0, 0, 0), (B1, 0, 0), (A1, 0, 0, 0), (B1, 0, 1), (A1, 0, 1, 0), (ARS, 0), (PR, 0, 0, 1), (A1, 0, 0, 1),
    (A2, 0, 0), (A1, 0, 1, 1), (B2, 0, 0, 0), (PR, 0, 0, 2), (B2, 0, 0, 1), (A2, 0, 1), (A1, 0, 1, 2), (PR, 1, 0, 0),
    (B1, 1, 0), (B2, 0, 1, 1), (A1, 0, 0, 2), (PR, 0, 0, 3), (A1, 1, 1, 0), (ARR, 0), (B2, 0, 1, 0), (B1, 1, 1),
    (A1, 0, 1, 3), (A3, 0, 1, 1), (B3, 0, 0), (PR, 1, 0, 1), (PR, 1, 0, 2), (A3, 0, 1, 0), (A1, 0, 0, 3),
    (PR, 1, 0, 3), (B3, 0, 1), (A1, 1, 1, 1), (A3, 0, 0, 0), (A3, 0, 0, 1), (B2, 1, 0, 1), (A1, 1, 0, 0), (ARH, 0),
    (B2, 1, 1, 0), (ARD, 0), (A1, 1, 1, 2), (FIN, 0, 1), (HS, 0, 1), (A2, 1, 1), (FIN, 0, 0), (HS, 0, 0),
    (B2, 1, 1, 1), (A1, 1, 0, 2), (A1, 1, 0, 1), (B2, 1, 0, 0), (A2, 1, 0), (A1, 1, 1, 3), (HW, 0, 1), (A1, 1, 0, 3),
    (G, 0, 1, 0), (G, 0, 1, 2), (G, 0, 1, 1), (HW, 0, 0), (G, 0, 0, 2), (BP, 0), (G, 0, 0, 0), (TH, 0, 0),
    (G, 0, 0, 1), (G, 0, 1, 3), (ARS, 1), (B3, 1, 1), (G, 0, 1, 6), (A3, 1, 0, 1), (G, 0, 1, 7), (G, 0, 0, 3),
    (G, 0, 1, 8), (A3, 1, 0, 0), (G, 0, 0, 4), (TK, 0, 0), (G, 0, 0, 8), (G, 0, 0, 9), (G, 0, 0, 7), (TH, 0, 1),
    (A3, 1, 1, 1), (TD, 0, 0), (G, 0, 1, 5), (G, 0, 1, 9), (G, 0, 0, 6), (B3, 1, 0), (G, 0, 0, 5), (ARR, 1),
    (G, 0, 1, 4), (A3, 1, 1, 0), (G, 0, 1, 12), (TK, 0, 1), (TD, 0, 1), (PR, 2, 0, 0), (A1, 2, 1, 0), (G, 0, 0, 12),
    (B1, 2, 0), (PR, 2, 0, 1), (PR, 2, 0, 2), (G, 0, 1, 11), (A1, 2, 0, 0), (A1, 2, 0, 1), (PR, 2, 0, 3), (B1, 2, 1),
    (G, 0, 0, 11), (G, 0, 0, 10), (A1, 2, 0, 2), (TH, 0, 2), (G, 0, 1, 10), (A1, 2, 1, 3), (ARH, 1), (FIN, 1, 1),
    (A1, 2, 1, 1), (B2, 2, 0, 0), (B2, 2, 0, 1), (TH, 0, 3), (A2, 2, 1), (TH, 0, 4), (A1, 2, 1, 2), (FIN, 1, 0),
    (TH, 0, 5), (A1, 2, 0, 3), (TK, 1, 0), (TH, 0, 6), (TH, 0, 7), (TD, 1, 0), (ARD, 1), (ACC, 0, 0), (CFIN, 0),
    (B2, 2, 1, 0), (B2, 2, 1, 1), (TK, 1, 1), (ACC, 0, 1), (TD, 1, 1), (ARS, 2), (CFIN, 1), (A2, 2, 0), (PR, 3, 0, 0),
    (B1, 3, 0), (A3, 2, 1, 0), (PR, 3, 0, 1), (A1, 3, 0, 1), (A3, 2, 1, 1), (ARR, 2), (B1, 3, 1), (B3, 2, 1),
    (A3, 2, 0, 1), (A3, 2, 0, 0), (B3, 2, 0), (B2, 3, 0, 0), (PR, 3, 0, 2), (PR, 3, 0, 3), (A1, 3, 0, 2),
    (B2, 3, 0, 1), (ARH, 2), (ARD, 2), (FIN, 2, 1), (HS, 1, 1), (A1, 3, 1, 1), (FIN, 2, 0), (HS, 1, 0), (B2, 3, 1, 0),
    (A1, 3, 1, 2), (B2, 3, 1, 1), (A1, 3, 0, 0), (B3, 3, 0), (HW, 1, 1), (G, 1, 1, 0), (G, 1, 1, 1), (A1, 3, 1, 0),
    (HW, 1, 0), (G, 1, 0, 0), (G, 1, 0, 1), (G, 1, 1, 2), (G, 1, 0, 2), (G, 1, 0, 3), (BP, 1), (GR, 0), (ARS, 3),
    (G, 1, 1, 3), (B3, 3, 1), (A2, 3, 1), (G, 1, 1, 7), (G, 1, 1, 6), (G, 1, 1, 4), (G, 1, 1, 5), (G, 1, 0, 6),
    (TH, 1, 0), (G, 1, 0, 4), (G, 1, 0, 9), (TH, 1, 1), (G, 1, 0, 8), (TH, 1, 2), (G, 1, 0, 7), (A1, 3, 0, 3),
    (G, 1, 1, 8), (TH, 1, 3), (G, 1, 0, 5), (G, 1, 1, 12), (A2, 3, 0), (ARR, 3), (A3, 3, 1, 0), (G, 1, 1, 9),
    (G, 1, 1, 10), (G, 1, 1, 11), (G, 1, 0, 12), (G, 1, 0, 11), (A1, 3, 1, 3), (G, 1, 0, 10), (TH, 1, 4),
    (A3, 3, 1, 1), (A3, 3, 0, 1), (A3, 3, 0, 0), (ARH, 3), (TH, 1, 5), (TH, 1, 6), (TH, 1, 7), (ACC, 1, 1),
    (ACC, 1, 0), (ARD, 3), (GR, 1), (FIN, 3, 0), (FIN, 3, 1), (END,),
)
PLAN_OTHERS = (
    (G, 0, 0, 0), (G, 0, 0, 2), (G, 0, 0, 1), (G, 0, 1, 3), (PR, 0, 0, 0), (B1, 0, 0), (B1, 0, 1), (PR, 0, 0, 1),
    (A1, 0, 0, 0), (A1, 0, 1, 0), (PR, 1, 0, 0), (ARS, 0), (A1, 1, 1, 0), (PR, 0, 0, 2), (PR, 1, 0, 1), (A1, 1, 0, 0),
    (B1, 1, 0), (G, 0, 0, 3), (G, 0, 0, 8), (A2, 0, 0), (A1, 0, 0, 2), (BP, 0), (A1, 0, 1, 2), (B2, 0, 0, 1),
    (B2, 0, 0, 0), (PR, 1, 0, 2), (A1, 1, 1, 2), (A1, 0, 0, 1), (ARR, 0), (B2, 0, 1, 0), (A2, 0, 1), (B2, 0, 1, 1),
    (B1, 1, 1), (PR, 0, 0, 3), (A1, 0, 1, 1), (A1, 1, 0, 1), (A2, 1, 1), (A1, 0, 0, 3), (PR, 1, 0, 3), (A2, 1, 0),
    (A3, 0, 0, 1), (A3, 0, 0, 0), (G, 0, 1, 0), (TH, 0, 0), (G, 0, 0, 9), (G, 0, 1, 2), (B3, 0, 0), (A1, 1, 1, 1),
    (A1, 1, 0, 3), (A3, 0, 1, 0), (G, 0, 1, 1), (A1, 1, 0, 2), (ARH, 0), (B3, 0, 1), (A3, 0, 1, 1), (ARD, 0),
    (B2, 1, 0, 0), (B2, 1, 0, 1), (A1, 0, 1, 3), (B2, 1, 1, 1), (B2, 1, 1, 0), (FIN, 0, 0), (A3, 1, 0, 1),
    (A3, 1, 1, 0), (TH, 0, 1), (G, 0, 1, 8), (FIN, 0, 1), (A3, 1, 0, 0), (A3, 1, 1, 1), (TH, 0, 2), (TH, 0, 3),
    (B3, 1, 0), (G, 0, 1, 4), (TK, 0, 0), (A1, 1, 1, 3), (G, 0, 0, 7), (G, 0, 1, 9), (G, 0, 1, 6), (G, 0, 0, 5),
    (G, 0, 1, 7), (G, 0, 1, 5), (B3, 1, 1), (ARS, 1), (G, 0, 0, 6), (TK, 0, 1), (FIN, 1, 0), (TD, 0, 0), (TD, 0, 1),
    (G, 0, 0, 4), (PR, 2, 0, 0), (PR, 2, 0, 1), (B1, 2, 1), (PR, 2, 0, 2), (FIN, 1, 1), (B1, 2, 0), (A1, 2, 0, 1),
    (TH, 0, 4), (G, 0, 0, 10), (A1, 2, 1, 0), (G, 0, 1, 10), (G, 0, 0, 11), (G, 0, 1, 11), (TK, 1, 0), (ARR, 1),
    (A1, 2, 0, 0), (A1, 2, 1, 2), (TD, 1, 0), (TH, 0, 5), (G, 0, 1, 12), (G, 0, 0, 12), (TH, 0, 6), (A1, 2, 1, 1),
    (B2, 2, 1, 1), (TK, 1, 1), (B2, 2, 1, 0), (TD, 1, 1), (PR, 3, 0, 0), (B1, 3, 0), (A1, 3, 0, 0), (A1, 3, 1, 0),
    (PR, 3, 0, 1), (PR, 3, 0, 2), (ARH, 1), (A1, 3, 0, 2), (A2, 2, 1), (B1, 3, 1), (ARD, 1), (A1, 3, 1, 2),
    (TH, 0, 7), (ACC, 0, 0), (ARS, 2), (A1, 3, 1, 1), (PR, 2, 0, 3), (B2, 2, 0, 0), (ACC, 0, 1), (GR, 0), (CFIN, 0),
    (B2, 2, 0, 1), (A1, 2, 1, 3), (CFIN, 1), (A2, 3, 0), (B2, 3, 1, 1), (A1, 3, 0, 1), (B2, 3, 1, 0), (PR, 3, 0, 3),
    (A1, 2, 0, 2), (ARR, 2), (CW, 0), (G, 1, 0, 2), (G, 1, 0, 1), (G, 1, 0, 0), (CW, 1), (G, 1, 1, 1), (G, 1, 1, 2),
    (G, 1, 0, 3), (G, 1, 1, 0), (A2, 2, 0), (BP, 1), (ARS, 3), (G, 1, 0, 9), (B3, 3, 1), (G, 1, 0, 6), (G, 1, 0, 7),
    (A1, 3, 0, 3), (A1, 3, 1, 3), (TH, 1, 0), (G, 1, 0, 5), (A2, 3, 1), (G, 1, 1, 5), (G, 1, 0, 4), (A3, 2, 1, 0),
    (G, 1, 1, 3), (G, 1, 1, 6), (G, 1, 1, 7), (B3, 2, 1), (B2, 3, 0, 1), (ARR, 3), (G, 1, 0, 12), (G, 1, 1, 4),
    (A3, 2, 1, 1), (B2, 3, 0, 0), (A1, 2, 0, 3), (TH, 1, 1), (G, 1, 0, 11), (G, 1, 0, 10), (G, 1, 1, 9), (G, 1, 0, 8),
    (ARH, 2), (ARD, 2), (TH, 1, 2), (G, 1, 1, 8), (TH, 1, 3), (G, 1, 1, 11), (TH, 1, 4), (G, 1, 1, 10), (A3, 2, 0, 1),
    (G, 1, 1, 12), (A3, 2, 0, 0), (A3, 3, 1, 1), (B3, 2, 0), (B3, 3, 0), (A3, 3, 0, 0), (A3, 3, 1, 0), (ARH, 3),
    (A3, 3, 0, 1), (TH, 1, 5), (TH, 1, 6), (TH, 1, 7), (ACC, 1, 1), (ARD, 3), (FIN, 2, 1), (ACC, 1, 0), (GR, 1),
    (FIN, 2, 0), (FIN, 3, 1), (FIN, 3, 0), (END,),
)


def nn(a, b):
    return lax.dot_general(a, b, (((1,), (0,)), ((), ())), preferred_element_type=F32)


def nt(a, b):
    return lax.dot_general(a, b, (((1,), (1,)), ((), ())), preferred_element_type=F32)


def tn(a, b):
    return lax.dot_general(a, b, (((0,), (0,)), ((), ())), preferred_element_type=F32)


def mixed(first, second):
    return (MIX_WEIGHT * first.astype(F32) + (1.0 - MIX_WEIGHT) * second.astype(F32)).astype(BF)


def split(first, count, more):
    up = (count // 16 + more) // 2 * 16
    return pl.ds(first, up), pl.ds(first + up, count - up)


def scratch(tok, cb, rank):
    rows, wide = 2 * tok, 2 * cb
    forward = [n for halves in ROWS_LAST[0] + ROWS_OTHERS[0] for n in halves]
    na, nb = max(forward), tok - min(forward)
    ha, hb = (na // 16 + 1) // 2 * 16, (nb // 16 + 1) // 2 * 16
    piece = tok // NT
    vm = lambda *shape: pltpu.VMEM(shape, BF)
    vf = lambda *shape: pltpu.VMEM(shape, F32)
    dma = lambda *shape: pltpu.SemaphoreType.DMA(shape)
    table = dict(
        wb=vm(NX, NY, wide, cb),
        xin=vm(4, rows, wide),
        st=vm(2, tok, wide),
        sb=vm(2, rows, cb),
        tg=vm(2, rows, cb),
        dn=vm(wide, rank),
        do=vm(wide, rank),
        dr=vm(wide, rank),
        ur=vm(rank, cb),
        ax=vf(2, 8, tok),
        pb=vm(4, NX, NY, rows, cb),
        ra1=vm(4, HALVES, 4, na, cb),
        ra2=vm(4, HALVES, 2, ha, cb),
        ra3=vm(4, HALVES, 2, na, cb),
        rb1=vm(4, HALVES, 2, NX, hb, cb),
        rb2=vm(4, HALVES, 2, NX, nb, cb),
        rb3=vm(4, HALVES, nb, cb),
        po=vm(4, rows, cb),
        gb=vm(2, NX, NY, rows, cb),
        gx=vm(tok, cb),
        acc=vf(2, rows, wide),
        bs=vm(HALVES, tok, cb),
        br=vm(HALVES, tok, cb),
        es=vm(tok, wide),
        er=vm(tok, wide),
        co=vm(rows, cb),
        bps=vm(2, rows, rank),
        bpr=vm(2, tok, rank),
        hi=vf(2, HALVES, 2 * NT, 8, tok),
        ls=[vm(tok, parts * rank) for parts in (4, 1, 2, 1)],
        ai=[vm(NT, piece, parts * rank) for parts in (4, 1, 2, 1)],
        ao=[vm(rows, parts * rank) for parts in (4, 1, 2, 1)],
        l_sem=dma(21),
        e_sem=[dma(21), dma(21)],
        r_sem=[dma(4, HALVES, 13), dma(4, HALVES, 13)],
        g_sem=[dma(2, HALVES, 13), dma(2, HALVES, 13)],
        a_sem=[dma(4, 3), dma(4, 3)],
        h_sem=[dma(2, HALVES), dma(2, HALVES)],
        p_sem=[dma(3, HALVES), dma(3, HALVES)],
        m_sem=[dma(12), dma(12)],
    )
    return table


def kernel(
    tree,
    sections,
    width,
    base_weight,
    pol_down,
    pol_up,
    old_down,
    old_up,
    pol_in,
    ref_in,
    grad_in,
    stash,
    fresh_pol,
    fresh_ref,
    targets,
    final_gain,
    token_side,
    ref_logratio,
    pol_out,
    ref_out,
    grad_out,
    grad_down,
    grad_up,
    *buffers,
):
    b = SimpleNamespace(**jax.tree.unflatten(tree, buffers))
    wb, xin, pb, gb, acc = b.wb, b.xin, b.pb, b.gb, b.acc
    rows, wide = xin.shape[1:]
    tok, cb = rows // 2, wide // 2
    rank = pol_up.shape[1]
    piece = tok // NT

    s = lax.axis_index("section")
    t = lax.axis_index("tensor")
    c = lax.axis_index("dp")
    x, y = t // NY, t % NY
    ox, oc = 1 - x, 1 - c
    ring = [(y + i) % NY for i in range(NY)]
    order = (ring[2], ring[1], ring[3], ring[0])
    y1, y2, y3 = ring[1:]
    is_last = s == sections - 1
    is_first = s == 0
    pair = (s, t, oc)
    over = (s, ox * NY + y, c)
    ways = ((s, x * NY + y1, c), (s, x * NY + y3, c))
    near = (y1, y3)

    my_rows = pl.ds(pl.multiple_of(c * tok, tok), tok)
    its_rows = pl.ds(pl.multiple_of(oc * tok, tok), tok)
    my_cols = pl.ds(pl.multiple_of(c * cb, cb), cb)
    its_cols = pl.ds(pl.multiple_of(oc * cb, cb), cb)

    def half(h):
        return pl.ds(h * tok, tok)

    def size(part):
        return pl.ds(0, part.size)

    def inner(part, h):
        return pl.ds(part.start - h * tok, part.size)

    def f32(ref, *index):
        return ref[index].astype(F32)

    def send(src, dst, group, index, device):
        return pltpu.make_async_remote_copy(
            src_ref=src,
            dst_ref=dst,
            send_sem=group[0].at[index],
            recv_sem=group[1].at[index],
            device_id=device,
            device_id_type=MESH,
        )

    def weight_cols(xx, yy, core):
        first = pl.multiple_of((xx * NY + yy) * wide + core * cb, cb)
        return base_weight.at[0, :, pl.ds(first, cb)]

    own, away, place = {}, {}, {}
    for j in range(4):
        for side in range(2):
            xx, yy, name = (ox, x)[side], order[j], ("w", j, side)
            own[name] = (weight_cols(xx, yy, c), wb.at[xx, yy, my_cols, :])
            away[name] = (weight_cols(xx, yy, oc), wb.at[xx, yy, my_cols, :])

    def both(name, src, dst):
        own[name] = away[name] = (src, dst)

    def columns(name, src, dst):
        own[name] = (src.at[:, my_cols], dst)
        away[name] = (src.at[:, its_cols], dst)

    both("dn", pol_down.at[0], b.dn.at[my_cols])
    both("do", old_down.at[0], b.do.at[my_cols])
    both("p0", pol_in.at[0], xin.at[0, my_rows])
    both("r0", ref_in.at[0], xin.at[1, my_rows])
    both("fp", fresh_pol.at[0], xin.at[2, my_rows])
    both("fr", fresh_ref.at[0], xin.at[3, my_rows])
    columns("g0", grad_in.at[0], gb.at[0, x, y, my_rows])
    columns("s0", stash.at[0, 0], b.sb.at[0, my_rows])
    columns("s1", stash.at[0, 1], b.sb.at[1, my_rows])
    columns("t0", targets.at[0], b.tg.at[0, my_rows])
    columns("t1", targets.at[1], b.tg.at[1, my_rows])
    own["st"] = (stash.at[0], b.st)
    away["ax"] = (b.ax.at[c], b.ax.at[c])
    for name in list(own) + ["ax"]:
        place[name] = len(place)

    def local(name):
        return pltpu.make_async_copy(*own[name], b.l_sem.at[place[name]])

    def swap(name):
        return send(*away[name], b.e_sem, place[name], pair)

    weights = [("w", j, side) for j in range(4) for side in range(2)]
    for name in ["p0", *weights[:2], "dn", "do", "g0", "r0", "st", *weights[2:], "s0", "s1", "t0", "t1"]:
        local(name).start()

    @pl.when(is_first)
    def _():
        local("fp").start()
        local("fr").start()

    me = 2 * t + c
    barrier = pltpu.get_barrier_semaphore()

    def greet(d, _):
        other = (me + d) % (2 * NT)
        pl.semaphore_signal(barrier, inc=1, device_id=(s, other // 2, other % 2), device_id_type=MESH)
        return 0

    after = ((s + 1) % sections, t, c)
    before = ((s + sections - 1) % sections, t, c)
    lax.fori_loop(1, 2 * NT, greet, 0)
    pl.semaphore_signal(barrier, inc=1, device_id=after, device_id_type=MESH)
    pl.semaphore_signal(barrier, inc=1, device_id=before, device_id_type=MESH)
    pl.semaphore_wait(barrier, 2 * NT + 1)

    for name in ["p0", *weights[:2], "g0", "dn", "do", *weights[2:4], "r0", *weights[4:]]:
        swap(name).start()

    side = token_side[...]
    signs = (side == 1).astype(F32) - (side == 2).astype(F32)
    ratios = jnp.concatenate([jnp.broadcast_to(ref_logratio[:, k : k + 1], (1, tok)) for k in range(2)], axis=0)
    b.ax[c] = jnp.concatenate([signs, ratios, signs, ratios], axis=0)
    for name in ("ax", "t0", "s0", "s1", "t1"):
        swap(name).start()

    @pl.when(is_first)
    def _():
        swap("fp").start()
        swap("fr").start()

    def schedule(plan, forward_rows, backward_rows, last):
        seen, sent = set(), []

        def need(*wanted):
            for name in wanted:
                if name in seen:
                    continue
                seen.add(name)
                if isinstance(name, tuple) and name[0] == "g":
                    g_copy(*name[1:]).wait_recv()
                    continue
                if name != "ax":
                    local(name).wait()
                if name != "st":
                    swap(name).wait_recv()
                    sent.append(swap(name))

        def start(copy):
            copy.start()
            sent.append(copy)

        def part_rows(index):
            return pl.ds(pl.multiple_of(index * piece, piece), piece)

        here = pl.ds(pl.multiple_of(c * tok + t * piece, piece), piece)

        def ars(i):
            ls, ai = b.ls[i], b.ai[i]
            if i == 0:
                need("dn", "do", "p0", "r0", "st")
                b.dr[...] = mixed(b.dn[...], b.do[...])
                b.ur[...] = mixed(pol_up[0], old_up[0])
                terms = (
                    (xin.at[0, my_rows], b.dn),
                    (xin.at[1, my_rows], b.dr),
                    (b.st.at[0], b.dn),
                    (b.st.at[1], b.dn),
                )
            elif i == 2:
                terms = ((xin.at[2, my_rows], b.dn), (xin.at[3, my_rows], b.dr))
            else:
                k = i // 2
                send(b.bps.at[k, its_rows], b.bpr.at[k], b.m_sem, k, pair).wait_recv()
                ls[...] = (f32(b.bps, k, my_rows) + f32(b.bpr, k)).astype(BF)
                terms = ()
            for q, (ref, down) in enumerate(terms):
                ls[:, q * rank : (q + 1) * rank] = nn(ref[...], down[...]).astype(BF)

            def one(d, _):
                tt = (t + d) % NT
                send(ls.at[part_rows(tt)], ai.at[t], b.a_sem, (i, 0), (s, tt, c)).start()
                return 0

            lax.fori_loop(1, NT, one, 0)
            ai[t] = ls[part_rows(t)]

        def arr(i):
            ai, ao = b.ai[i], b.ao[i]
            seven = ai.at[pl.ds(0, NT - 1)]
            pltpu.make_async_copy(seven, seven, b.a_sem[1].at[i, 0]).wait()
            total = ai[0].astype(F32)
            for d in range(1, NT):
                total += ai[d].astype(F32)
            ao[here] = total.astype(BF)

            def one(d, _):
                tt = (t + d) % NT
                send(ao.at[here], ao.at[here], b.a_sem, (i, 1), (s, tt, c)).start()
                return 0

            lax.fori_loop(1, NT, one, 0)

        def arh(i):
            ao = b.ao[i]
            most = ao.at[pl.ds(0, piece * (NT - 1))]
            pltpu.make_async_copy(most, most, b.a_sem[1].at[i, 1]).wait()
            start(send(ao.at[my_rows], ao.at[my_rows], b.a_sem, (i, 2), pair))

        def ard(i):
            ao = b.ao[i]
            send(ao.at[my_rows], ao.at[my_rows], b.a_sem, (i, 2), pair).wait_recv()

        def sums_sent(i):
            seven = b.ai[i].at[pl.ds(0, NT - 1)]
            pltpu.make_async_copy(seven, seven, b.a_sem[0].at[i, 0]).wait()
            most = b.ao[i].at[pl.ds(0, piece * (NT - 1))]
            pltpu.make_async_copy(most, most, b.a_sem[0].at[i, 1]).wait()

        def a_part(p, h):
            return pl.ds(h * tok, forward_rows[p][h])

        def b_part(p, h):
            return pl.ds(h * tok + forward_rows[p][h], tok - forward_rows[p][h])

        def a_half(p, h, up):
            part = a_part(p, h)
            return split(part.start, part.size, 1)[up]

        def b_half(p, h, up):
            part = b_part(p, h)
            return split(part.start, part.size, 0)[up]

        def c_a1(p, h, j):
            part = a_part(p, h)
            return send(pb.at[p, ox, order[j], part], b.ra1.at[p, h, j, size(part)], b.r_sem, (p, h, j), over)

        def c_a2(p, h, up):
            part = a_half(p, h, up)
            return send(pb.at[p, x, y2, part], b.ra2.at[p, h, up, size(part)], b.r_sem, (p, h, 4 + up), ways[up])

        def c_b1(p, h, up):
            part = b_half(p, h, up)
            return send(pb.at[p, :, y2, part], b.rb1.at[p, h, up, :, size(part)], b.r_sem, (p, h, 6 + up), ways[up])

        def c_b2(p, h, up):
            part = b_part(p, h)
            return send(pb.at[p, :, near[up], part], b.rb2.at[p, h, up, :, size(part)], b.r_sem, (p, h, 8 + up), ways[up])

        def c_b3(p, h):
            part = b_part(p, h)
            return send(pb.at[p, ox, y, part], b.rb3.at[p, h, size(part)], b.r_sem, (p, h, 10), over)

        def c_a3(p, h, up):
            part = a_part(p, h)
            return send(pb.at[p, x, near[up], part], b.ra3.at[p, h, up, size(part)], b.r_sem, (p, h, 11 + up), ways[up])

        def pr(p, _, j):
            if p < 2:
                need(("p0", "r0")[p])
            need(("w", j, 0), ("w", j, 1))
            for xx in (ox, x):
                pb[p, xx, order[j]] = nn(xin[p], wb[xx, order[j]]).astype(BF)

        def a1(p, h, j):
            start(c_a1(p, h, j))

        def b1(p, h):
            start(c_b1(p, h, 0))
            start(c_b1(p, h, 1))

        def b2(p, h, up):
            part, yy = b_half(p, h, up), near[up]
            c_b1(p, h, up).wait_recv()
            for xx in range(NX):
                pb[p, xx, yy, part] = (f32(pb, p, xx, yy, part) + f32(b.rb1, p, h, up, xx, size(part))).astype(BF)
            start(c_b2(p, h, up))

        def a2(p, h):
            part = a_part(p, h)
            c_a1(p, h, 0).wait_recv()
            pb[p, x, y2, part] = (f32(pb, p, x, y2, part) + f32(b.ra1, p, h, 0, size(part))).astype(BF)
            start(c_a2(p, h, 0))
            start(c_a2(p, h, 1))

        def b3(p, h):
            part = b_part(p, h)
            n = size(part)
            c_b2(p, h, 0).wait_recv()
            c_b2(p, h, 1).wait_recv()
            pb[p, ox, y, part] = (
                f32(pb, p, ox, y, part) + f32(b.rb2, p, h, 0, ox, n) + f32(b.rb2, p, h, 1, ox, n)
            ).astype(BF)
            start(c_b3(p, h))

        def a3(p, h, up):
            yy, part, rest = near[up], a_half(p, h, up), a_half(p, h, 1 - up)
            c_a1(p, h, 1 + up).wait_recv()
            c_a2(p, h, up).wait_recv()
            pb[p, x, yy, part] = (
                f32(pb, p, x, yy, part)
                + f32(b.ra1, p, h, 1 + up, inner(part, h))
                + f32(b.ra2, p, h, up, size(part))
            ).astype(BF)
            pb[p, x, yy, rest] = (f32(pb, p, x, yy, rest) + f32(b.ra1, p, h, 1 + up, inner(rest, h))).astype(BF)
            start(c_a3(p, h, up))

        def fin(p, h):
            c_a1(p, h, 3).wait_recv()
            c_a3(p, h, 0).wait_recv()
            c_a3(p, h, 1).wait_recv()
            c_b3(p, h).wait_recv()
            low, up_ref = b.ao[p // 2 * 2], (pol_up[0], b.ur[...])[p % 2]
            low_cols = pl.ds(p % 2 * rank, rank)
            a, bb = a_part(p, h), b_part(p, h)
            na, nb = size(a), size(bb)
            summed = (
                f32(pb, p, x, y, a) + f32(b.ra1, p, h, 3, na) + f32(b.ra3, p, h, 0, na) + f32(b.ra3, p, h, 1, na),
                f32(pb, p, x, y, bb)
                + f32(b.rb2, p, h, 0, x, nb)
                + f32(b.rb2, p, h, 1, x, nb)
                + f32(b.rb3, p, h, nb),
            )
            for part, total in zip((a, bb), summed):
                adapted = ADAPTER_SCALE * nn(low[part, low_cols], up_ref)
                b.po[p, part] = (f32(xin, p, part, my_cols) + total + adapted).astype(BF)
            if p < 2:
                if not last:
                    start(c_pass(p, h))
                return
            out = (pol_out, ref_out)[p - 2]

            @pl.when(c == h)
            def _():
                out[0, :, my_cols] = b.po[p, half(h)]

            @pl.when(c != h)
            def _():
                c_out(p, h).start()

        def c_out(p, h):
            return send(b.po.at[p, half(h)], (pol_out, ref_out)[p - 2].at[0, :, my_cols], b.m_sem, p, pair)

        def c_pass(i, h):
            if i < 2:
                return send(b.po.at[i, half(h)], xin.at[2 + i, half(h), my_cols], b.p_sem, (i, h), after)
            return send(b.co.at[half(h)], gb.at[1, x, y, half(h)], b.p_sem, (2, h), before)

        def c_take(i, h):
            block = xin.at[2 + i, half(h), my_cols]
            return send(block, block, b.m_sem, 4 + 2 * i + h, pair)

        def unless_first(body):
            if last:
                body()
            else:
                pl.when(jnp.logical_not(is_first))(body)

        def tk(i, h):
            @unless_first
            def _():
                c_pass(i, h).wait_recv()
                c_take(i, h).start()

        def td(i, h):
            @unless_first
            def _():
                c_take(i, h).wait()

            if not last and ("fresh", i) not in seen:
                seen.add(("fresh", i))

                @pl.when(is_first)
                def _():
                    local(("fp", "fr")[i]).wait()
                    swap(("fp", "fr")[i]).wait()

        def hs(k, h):
            need(("t0", "t1")[k])
            p, part = 2 * k, half(h)
            gain = final_gain[:, my_cols]
            hidden = f32(b.po, p, part)
            squares = jnp.sum(hidden * hidden, axis=1, keepdims=True)
            inner_sum = jnp.sum(hidden * gain * f32(b.tg, k, part), axis=1, keepdims=True)
            lane = lax.broadcasted_iota(jnp.int32, (tok, 128), 1)
            b.hi[k, h, me] = jnp.where(lane == 0, squares, inner_sum).T[:8]

            def one(d, _):
                other = (me + d) % (2 * NT)
                slot = b.hi.at[k, h, me]
                send(slot, slot, b.h_sem, (k, h), (s, other // 2, other % 2)).start()
                return 0

            lax.fori_loop(1, 2 * NT, one, 0)

        def hw(k, h):
            if k == 0:
                need("g0")
            need("ax")
            others = b.hi.at[k, h, pl.ds(0, 2 * NT - 1)]
            pltpu.make_async_copy(others, others, b.h_sem[1].at[k, h]).wait()
            total = b.hi[k, h, 0]
            for d in range(1, 2 * NT):
                total += b.hi[k, h, d]
            sums = jnp.concatenate([total] * 16, axis=0).T
            squares, dot = sums[:, 0:1], sums[:, 1:2]
            r = lax.rsqrt(squares / width + NORM_EPSILON)
            aux = jnp.concatenate([b.ax[h]] * 16, axis=0).T
            sign, ratio = aux[:, k : k + 1], aux[0:1, 2 + k : 3 + k]
            margin = PREF_BETA * (jnp.sum(dot * r * sign, axis=0, keepdims=True) - ratio)
            weight = -LOSS_SCALE * PREF_BETA * jax.nn.sigmoid(-margin) * sign
            gain = final_gain[:, my_cols]
            hidden, target = f32(b.po, 2 * k, half(h)), f32(b.tg, k, half(h))
            g = weight * (r * gain * target - (dot * r * r * r / width) * hidden)
            gb[k, x, y, half(h)] = g.astype(BF)

        def head_sent(k, h):
            others = b.hi.at[k, h, pl.ds(0, 2 * NT - 1)]
            pltpu.make_async_copy(others, others, b.h_sem[0].at[k, h]).wait()

        routes = ((), (), (), (), (2,), (2,), (0,), (1,), (0,), (1,), (4,), (5,), (6, 7))

        def g_copy(k, h, i):
            n = backward_rows[k][h]
            first = h * tok
            a, bb = pl.ds(first, n), pl.ds(first + n, tok - n)
            low, high = split(first, tok, 0)
            a_low, a_high = split(first, n, 0)
            xx, yy, part, device = (
                (x, y, half(h), ways[0]),
                (x, y, half(h), ways[1]),
                (x, y, a, over),
                (x, y, bb, over),
                (ox, y, a, ways[0]),
                (ox, y, a, ways[1]),
                (x, y3, low, ways[0]),
                (x, y1, high, ways[1]),
                (x, y3, bb, over),
                (x, y1, bb, over),
                (ox, y3, a_low, ways[0]),
                (ox, y1, a_high, ways[1]),
                (x, y2, bb, over),
            )[i]
            block = gb.at[k, xx, yy, part]
            return send(block, block, b.g_sem, (k, h, i), device)

        def g(k, h, i):
            if k == 0 and not last:
                need("g0")
            need(*[("g", k, h, q) for q in routes[i]])
            start(g_copy(k, h, i))

        def th(k, q):
            need(*weights)
            if k == 0 and not last:
                need("g0")
            xx, yy, wanted = (
                (x, y, ()),
                (x, y3, (0,)),
                (x, y1, (1,)),
                (ox, y, (2, 3)),
                (x, y2, (6, 7)),
                (ox, y3, (4, 8)),
                (ox, y1, (5, 9)),
                (ox, y2, (10, 11, 12)),
            )[q]
            need(*[("g", k, h, i) for h in range(HALVES) for i in wanted])
            term = nt(gb[k, xx, yy], wb[xx, yy])
            acc[k] = term if q == 0 else acc[k] + term

        def c_acc(h):
            return send(b.bs.at[h], b.br.at[h], b.m_sem, 8 + h, pair)

        def c_end():
            return send(b.es, b.er, b.m_sem, 10, pair)

        def c_gx():
            return send(gb.at[1, x, y, its_rows], b.gx, b.m_sem, 11, pair)

        def acc_(k, h):
            if k == 0:
                b.bs[h] = acc[0, half(h), its_cols].astype(BF)
                start(c_acc(h))
            else:

                @pl.when(c != h)
                def _():
                    b.es[...] = acc[1, half(h)].astype(BF)
                    c_end().start()

        def bp(k):
            if k == 0 and not last:
                need("g0")
            b.bps[k] = nt(gb[k, x, y], pol_up[0]).astype(BF)
            start(send(b.bps.at[k, its_rows], b.bpr.at[k], b.m_sem, k, pair))
            if k == 1:
                start(c_gx())

        def cfin(h):
            c_acc(h).wait_recv()
            back = b.ao[1][half(h)]
            adapted = ADAPTER_SCALE * nt(back, b.dn[my_cols])
            total = f32(gb, 0, x, y, half(h)) + acc[0, half(h), my_cols] + f32(b.br, h)
            b.co[half(h)] = (total + adapted).astype(BF)
            if last:
                start(c_pass(2, h))
            else:

                @pl.when(jnp.logical_not(is_first))
                def _():
                    c_pass(2, h).start()

        def cw(h):
            c_pass(2, h).wait_recv()

        def gr(k):
            need("s0", "s1")
            back = b.ao[2 * k + 1][...]
            if last:
                stored, low = xin[2 * k, :, my_cols], b.ao[2 * k][:, 0:rank]
            else:
                stored, low = b.sb[k], b.ao[0][:, (2 + k) * rank : (3 + k) * rank]
            down = ADAPTER_SCALE * tn(stored, back)
            up = ADAPTER_SCALE * tn(low, gb[k, x, y])
            if k == 0:
                grad_down[0] = down
                grad_up[0] = up
            else:
                grad_down[0] += down
                grad_up[0] += up

        def end():
            c_gx().wait_recv()
            c_end().wait_recv()
            back = b.ao[3][my_rows]
            for cols, cotangent in ((my_cols, gb.at[1, x, y, my_rows]), (its_cols, b.gx)):
                adapted = ADAPTER_SCALE * nt(back, b.dn[cols])
                total = cotangent[...].astype(F32) + acc[1, my_rows, cols] + b.er[:, cols].astype(F32)
                grad_out[0, :, cols] = (total + adapted).astype(BF)
            need(*[name for name in place if name not in ("fp", "fr")])
            for p in (2, 3):
                c_out(p, 0).wait()
            c_end().wait_send()
            for copy in sent:
                copy.wait_send()
            if not last:

                @unless_first
                def _():
                    for h in range(HALVES):
                        c_pass(2, h).wait_send()

            for i in range(4):
                sums_sent(i)
            if last:
                for k in range(2):
                    for h in range(HALVES):
                        head_sent(k, h)

        steps = (
            pr, a1, a2, a3, b1, b2, b3, fin, ars, arr, arh, ard, hs, hw, g, th, bp, acc_, cfin, cw, tk, td, gr, end
        )
        for step, *index in plan:
            steps[step](*index)

    @pl.when(is_last)
    def _():
        schedule(PLAN_LAST, *ROWS_LAST, True)

    @pl.when(jnp.logical_not(is_last))
    def _():
        schedule(PLAN_OTHERS, *ROWS_OTHERS, False)


def put(*refs):
    copies = [pltpu.make_async_copy(refs[i], refs[5 + i], refs[10].at[i]) for i in range(5)]
    for copy in copies:
        copy.start()
    for copy in copies:
        copy.wait()


def on_device(sections, width, *operands):
    pol_in = operands[5]
    tok, wide = pol_in.shape[1:]
    cb = wide // 2
    rank = operands[1].shape[2]
    operands = list(operands)
    operands[12] = operands[12].reshape(1, wide)
    operands[14] = operands[14].reshape(1, 2)
    buffers, tree = jax.tree.flatten(scratch(tok, cb, rank))
    anywhere = pl.BlockSpec(memory_space=pl.ANY)
    inside = pl.BlockSpec(memory_space=pltpu.VMEM)
    in_vmem = (2, 4, 12, 13, 14)
    outs = (
        jax.ShapeDtypeStruct((1, tok, wide), BF),
        jax.ShapeDtypeStruct((1, tok, wide), BF),
        jax.ShapeDtypeStruct((1, tok, wide), BF),
        jax.ShapeDtypeStruct((1, cb, rank), F32),
        jax.ShapeDtypeStruct((1, rank, cb), F32),
    )
    results = pl.pallas_call(
        functools.partial(kernel, tree, sections, width),
        out_shape=outs,
        in_specs=[inside if i in in_vmem else anywhere for i in range(15)],
        out_specs=[inside] * 5,
        scratch_shapes=buffers,
        compiler_params=pltpu.CompilerParams(
            collective_id=0, has_side_effects=True, vmem_limit_bytes=56 * 1024 * 1024
        ),
        name="relay",
    )(*operands)
    return pl.pallas_call(
        put,
        out_shape=outs,
        in_specs=[inside] * 5,
        out_specs=[anywhere] * 5,
        scratch_shapes=[pltpu.SemaphoreType.DMA((5,))],
        name="put",
    )(*results)


def solution(mesh):
    in_specs = (
        P("section", ("tensor", "dp"), None),
        P("section", ("tensor", "dp"), None),
        P("section", None, ("tensor", "dp")),
        P("section", ("tensor", "dp"), None),
        P("section", None, ("tensor", "dp")),
        P("section", "dp", "tensor"),
        P("section", "dp", "tensor"),
        P("section", "dp", "tensor"),
        P("section", None, "dp", "tensor"),
        P(None, "dp", "tensor"),
        P(None, "dp", "tensor"),
        P(None, "dp", "tensor"),
        P("tensor"),
        P(None, "dp"),
        P(None, "dp"),
    )
    out_specs = (
        P("section", "dp", "tensor"),
        P("section", "dp", "tensor"),
        P("section", "dp", "tensor"),
        P("section", ("tensor", "dp"), None),
        P("section", None, ("tensor", "dp")),
    )
    sections = mesh.shape["section"]

    def whole(base_weight, *rest):
        body = functools.partial(on_device, sections, base_weight.shape[1])
        return jax.shard_map(
            body, mesh=mesh, in_specs=in_specs, out_specs=out_specs, check_vma=False
        )(base_weight, *rest)

    return whole
```

```python
import functools
from types import SimpleNamespace

import jax
import jax.numpy as jnp
from jax import lax
from jax.experimental import pallas as pl
from jax.experimental.pallas import tpu as pltpu
from jax.sharding import PartitionSpec as P

BF = jnp.bfloat16
F32 = jnp.float32
MESH = pl.DeviceIdType.MESH

NX, NY = 2, 4
NT = NX * NY
HALVES = 2
ROWS_LAST = (((48, 64), (80, 48), (32, 64), (32, 48)), ((80, 80), (64, 96)))
ROWS_OTHERS = (((32, 64), (48, 32), (64, 32), (48, 48)), ((112, 80), (80, 96)))

ADAPTER_SCALE = 0.5
MIX_WEIGHT = 0.6
PREF_BETA = 0.1
LOSS_SCALE = 1024.0
NORM_EPSILON = 1e-06

PR, A1, A2, A3, B1, B2, B3, FIN, ARS, ARR, ARH, ARD,     HS, HW, G, TH, BP, ACC, CFIN, CW, TK, TD, GR, END = range(24)
PLAN_LAST = (
    (PR, 0, 0, 0), (B1, 0, 0), (A1, 0, 1, 0), (A1, 0, 0, 0), (ARS, 0), (B1, 0, 1), (PR, 0, 0, 1), (A1, 0, 0, 1),
    (PR, 1, 0, 0), (A1, 1, 1, 0), (B1, 1, 1), (PR, 0, 0, 2), (A1, 0, 1, 1), (B2, 0, 0, 1), (A2, 0, 1), (PR, 1, 0, 1),
    (A1, 1, 1, 1), (A2, 0, 0), (B2, 0, 0, 0), (B2, 0, 1, 1), (PR, 0, 0, 3), (A1, 0, 1, 2), (A1, 0, 0, 2),
    (A1, 0, 0, 3), (B2, 0, 1, 0), (ARR, 0), (PR, 1, 0, 2), (B1, 1, 0), (A3, 0, 1, 0), (A1, 1, 1, 2), (A1, 1, 0, 0),
    (A3, 0, 0, 0), (A2, 1, 1), (B3, 0, 0), (PR, 1, 0, 3), (A1, 0, 1, 3), (B2, 1, 1, 0), (B3, 0, 1), (A3, 0, 0, 1),
    (A3, 0, 1, 1), (B2, 1, 0, 1), (ARH, 0), (A1, 1, 0, 2), (A3, 1, 1, 1), (ARD, 0), (FIN, 0, 0), (HS, 0, 0),
    (A2, 1, 0), (A1, 1, 1, 3), (FIN, 0, 1), (HS, 0, 1), (A3, 1, 1, 0), (B2, 1, 1, 1), (A1, 1, 0, 3), (B2, 1, 0, 0),
    (A1, 1, 0, 1), (HW, 0, 0), (G, 0, 0, 0), (G, 0, 0, 2), (A3, 1, 0, 1), (HW, 0, 1), (G, 0, 1, 3), (G, 0, 1, 1),
    (TH, 0, 0), (BP, 0), (G, 0, 1, 2), (G, 0, 1, 0), (G, 0, 0, 1), (ARS, 1), (A3, 1, 0, 0), (B3, 1, 0), (G, 0, 0, 3),
    (G, 0, 0, 4), (TK, 0, 0), (G, 0, 0, 5), (G, 0, 1, 9), (TH, 0, 1), (G, 0, 1, 7), (B3, 1, 1), (G, 0, 1, 4),
    (G, 0, 1, 6), (G, 0, 1, 8), (G, 0, 0, 9), (G, 0, 1, 5), (TK, 0, 1), (G, 0, 0, 7), (FIN, 1, 0), (G, 0, 0, 8),
    (TH, 0, 2), (TD, 0, 1), (TD, 0, 0), (ARR, 1), (G, 0, 0, 6), (PR, 2, 0, 0), (B1, 2, 0), (PR, 2, 0, 1),
    (A1, 2, 1, 0), (A1, 2, 0, 0), (B1, 2, 1), (G, 0, 1, 12), (PR, 2, 0, 2), (G, 0, 1, 11), (TH, 0, 3), (PR, 2, 0, 3),
    (A1, 2, 0, 3), (G, 0, 0, 10), (G, 0, 0, 12), (A1, 2, 1, 2), (G, 0, 0, 11), (G, 0, 1, 10), (A1, 2, 0, 2),
    (TH, 0, 4), (A1, 2, 1, 3), (B2, 2, 0, 0), (ARH, 1), (A1, 2, 1, 1), (B2, 2, 0, 1), (TH, 0, 5), (B2, 2, 1, 1),
    (TH, 0, 6), (ARD, 1), (FIN, 1, 1), (TK, 1, 0), (TD, 1, 0), (B2, 2, 1, 0), (TH, 0, 7), (ACC, 0, 0), (ACC, 0, 1),
    (TK, 1, 1), (CFIN, 0), (TD, 1, 1), (ARS, 2), (GR, 0), (A2, 2, 0), (A1, 2, 0, 1), (A2, 2, 1), (PR, 3, 0, 0),
    (CFIN, 1), (B1, 3, 0), (PR, 3, 0, 1), (B1, 3, 1), (ARR, 2), (A3, 2, 1, 1), (B3, 2, 1), (B3, 2, 0), (A3, 2, 1, 0),
    (A3, 2, 0, 0), (A1, 3, 0, 0), (A1, 3, 1, 0), (A3, 2, 0, 1), (PR, 3, 0, 2), (PR, 3, 0, 3), (B2, 3, 0, 0),
    (B2, 3, 0, 1), (ARH, 2), (A1, 3, 0, 3), (ARD, 2), (FIN, 2, 1), (HS, 1, 1), (FIN, 2, 0), (A1, 3, 0, 2), (HS, 1, 0),
    (B2, 3, 1, 0), (A1, 3, 1, 3), (A2, 3, 0), (A1, 3, 1, 2), (B2, 3, 1, 1), (A1, 3, 1, 1), (A1, 3, 0, 1), (HW, 1, 1),
    (G, 1, 1, 0), (G, 1, 1, 2), (G, 1, 1, 1), (HW, 1, 0), (BP, 1), (G, 1, 0, 1), (G, 1, 0, 3), (TH, 1, 0),
    (G, 1, 1, 3), (G, 1, 0, 0), (G, 1, 0, 2), (ARS, 3), (B3, 3, 0), (G, 1, 1, 5), (G, 1, 1, 4), (G, 1, 1, 6),
    (G, 1, 1, 7), (G, 1, 1, 8), (G, 1, 1, 9), (G, 1, 0, 6), (G, 1, 0, 9), (G, 1, 0, 8), (TH, 1, 1), (G, 1, 0, 4),
    (G, 1, 0, 7), (G, 1, 0, 5), (ARR, 3), (TH, 1, 2), (G, 1, 1, 12), (A2, 3, 1), (G, 1, 1, 11), (TH, 1, 3),
    (G, 1, 1, 10), (G, 1, 0, 12), (A3, 3, 0, 0), (TH, 1, 4), (G, 1, 0, 11), (G, 1, 0, 10), (B3, 3, 1), (TH, 1, 5),
    (A3, 3, 0, 1), (A3, 3, 1, 1), (ARH, 3), (A3, 3, 1, 0), (TH, 1, 6), (ARD, 3), (TH, 1, 7), (ACC, 1, 1), (ACC, 1, 0),
    (FIN, 3, 0), (GR, 1), (FIN, 3, 1), (END,),
)
PLAN_OTHERS = (
    (G, 0, 0, 0), (G, 0, 0, 2), (G, 0, 0, 1), (G, 0, 1, 3), (PR, 0, 0, 0), (B1, 0, 0), (B1, 0, 1), (PR, 0, 0, 1),
    (A1, 0, 0, 0), (A1, 0, 1, 0), (PR, 1, 0, 0), (ARS, 0), (A1, 1, 1, 0), (PR, 0, 0, 2), (PR, 1, 0, 1), (A1, 1, 0, 0),
    (B1, 1, 0), (G, 0, 0, 3), (G, 0, 0, 8), (A2, 0, 0), (A1, 0, 0, 2), (BP, 0), (A1, 0, 1, 2), (B2, 0, 0, 1),
    (B2, 0, 0, 0), (PR, 1, 0, 2), (A1, 1, 1, 2), (A1, 0, 0, 1), (ARR, 0), (B2, 0, 1, 0), (A2, 0, 1), (B2, 0, 1, 1),
    (B1, 1, 1), (PR, 0, 0, 3), (A1, 0, 1, 1), (A1, 1, 0, 1), (A2, 1, 1), (A1, 0, 0, 3), (PR, 1, 0, 3), (A2, 1, 0),
    (A3, 0, 0, 1), (A3, 0, 0, 0), (G, 0, 1, 0), (TH, 0, 0), (G, 0, 0, 9), (G, 0, 1, 2), (B3, 0, 0), (A1, 1, 1, 1),
    (A1, 1, 0, 3), (A3, 0, 1, 0), (G, 0, 1, 1), (A1, 1, 0, 2), (ARH, 0), (B3, 0, 1), (A3, 0, 1, 1), (ARD, 0),
    (B2, 1, 0, 0), (B2, 1, 0, 1), (A1, 0, 1, 3), (B2, 1, 1, 1), (B2, 1, 1, 0), (FIN, 0, 0), (A3, 1, 0, 1),
    (A3, 1, 1, 0), (TH, 0, 1), (G, 0, 1, 8), (FIN, 0, 1), (A3, 1, 0, 0), (A3, 1, 1, 1), (TH, 0, 2), (TH, 0, 3),
    (B3, 1, 0), (G, 0, 1, 4), (TK, 0, 0), (A1, 1, 1, 3), (G, 0, 0, 7), (G, 0, 1, 9), (G, 0, 1, 6), (G, 0, 0, 5),
    (G, 0, 1, 7), (G, 0, 1, 5), (B3, 1, 1), (ARS, 1), (G, 0, 0, 6), (TK, 0, 1), (FIN, 1, 0), (TD, 0, 0), (TD, 0, 1),
    (G, 0, 0, 4), (PR, 2, 0, 0), (PR, 2, 0, 1), (B1, 2, 1), (PR, 2, 0, 2), (FIN, 1, 1), (B1, 2, 0), (A1, 2, 0, 1),
    (TH, 0, 4), (G, 0, 0, 10), (A1, 2, 1, 0), (G, 0, 1, 10), (G, 0, 0, 11), (G, 0, 1, 11), (TK, 1, 0), (ARR, 1),
    (A1, 2, 0, 0), (A1, 2, 1, 2), (TD, 1, 0), (TH, 0, 5), (G, 0, 1, 12), (G, 0, 0, 12), (TH, 0, 6), (A1, 2, 1, 1),
    (B2, 2, 1, 1), (TK, 1, 1), (B2, 2, 1, 0), (TD, 1, 1), (PR, 3, 0, 0), (B1, 3, 0), (A1, 3, 0, 0), (A1, 3, 1, 0),
    (PR, 3, 0, 1), (PR, 3, 0, 2), (ARH, 1), (A1, 3, 0, 2), (A2, 2, 1), (B1, 3, 1), (ARD, 1), (A1, 3, 1, 2),
    (TH, 0, 7), (ACC, 0, 0), (ARS, 2), (A1, 3, 1, 1), (PR, 2, 0, 3), (B2, 2, 0, 0), (ACC, 0, 1), (GR, 0), (CFIN, 0),
    (B2, 2, 0, 1), (A1, 2, 1, 3), (CFIN, 1), (A2, 3, 0), (B2, 3, 1, 1), (A1, 3, 0, 1), (B2, 3, 1, 0), (PR, 3, 0, 3),
    (A1, 2, 0, 2), (ARR, 2), (CW, 0), (G, 1, 0, 2), (G, 1, 0, 1), (G, 1, 0, 0), (CW, 1), (G, 1, 1, 1), (G, 1, 1, 2),
    (G, 1, 0, 3), (G, 1, 1, 0), (A2, 2, 0), (BP, 1), (ARS, 3), (G, 1, 0, 9), (B3, 3, 1), (G, 1, 0, 6), (G, 1, 0, 7),
    (A1, 3, 0, 3), (A1, 3, 1, 3), (TH, 1, 0), (G, 1, 0, 5), (A2, 3, 1), (G, 1, 1, 5), (G, 1, 0, 4), (A3, 2, 1, 0),
    (G, 1, 1, 3), (G, 1, 1, 6), (G, 1, 1, 7), (B3, 2, 1), (B2, 3, 0, 1), (ARR, 3), (G, 1, 0, 12), (G, 1, 1, 4),
    (A3, 2, 1, 1), (B2, 3, 0, 0), (A1, 2, 0, 3), (TH, 1, 1), (G, 1, 0, 11), (G, 1, 0, 10), (G, 1, 1, 9), (G, 1, 0, 8),
    (ARH, 2), (ARD, 2), (TH, 1, 2), (G, 1, 1, 8), (TH, 1, 3), (G, 1, 1, 11), (TH, 1, 4), (G, 1, 1, 10), (A3, 2, 0, 1),
    (G, 1, 1, 12), (A3, 2, 0, 0), (A3, 3, 1, 1), (B3, 2, 0), (B3, 3, 0), (A3, 3, 0, 0), (A3, 3, 1, 0), (ARH, 3),
    (A3, 3, 0, 1), (TH, 1, 5), (TH, 1, 6), (TH, 1, 7), (ACC, 1, 1), (ARD, 3), (FIN, 2, 1), (ACC, 1, 0), (GR, 1),
    (FIN, 2, 0), (FIN, 3, 1), (FIN, 3, 0), (END,),
)


def nn(a, b):
    return lax.dot_general(a, b, (((1,), (0,)), ((), ())), preferred_element_type=F32)


def nt(a, b):
    return lax.dot_general(a, b, (((1,), (1,)), ((), ())), preferred_element_type=F32)


def tn(a, b):
    return lax.dot_general(a, b, (((0,), (0,)), ((), ())), preferred_element_type=F32)


def mixed(first, second):
    return (MIX_WEIGHT * first.astype(F32) + (1.0 - MIX_WEIGHT) * second.astype(F32)).astype(BF)


def split(first, count, more):
    up = (count // 16 + more) // 2 * 16
    return pl.ds(first, up), pl.ds(first + up, count - up)


def scratch(tok, cb, rank):
    rows, wide = 2 * tok, 2 * cb
    forward = [n for halves in ROWS_LAST[0] + ROWS_OTHERS[0] for n in halves]
    na, nb = max(forward), tok - min(forward)
    ha, hb = (na // 16 + 1) // 2 * 16, (nb // 16 + 1) // 2 * 16
    piece = tok // NT
    vm = lambda *shape: pltpu.VMEM(shape, BF)
    vf = lambda *shape: pltpu.VMEM(shape, F32)
    dma = lambda *shape: pltpu.SemaphoreType.DMA(shape)
    table = dict(
        wb=vm(NX, NY, wide, cb),
        xin=vm(4, rows, wide),
        st=vm(2, tok, wide),
        sb=vm(2, rows, cb),
        tg=vm(2, rows, cb),
        dn=vm(wide, rank),
        do=vm(wide, rank),
        dr=vm(wide, rank),
        up=vm(rank, cb),
        ou=vm(rank, cb),
        ur=vm(rank, cb),
        ax=vf(2, 8, tok),
        pb=vm(4, NX, NY, rows, cb),
        ra1=vm(4, HALVES, 4, na, cb),
        ra2=vm(4, HALVES, 2, ha, cb),
        ra3=vm(4, HALVES, 2, na, cb),
        rb1=vm(4, HALVES, 2, NX, hb, cb),
        rb2=vm(4, HALVES, 2, NX, nb, cb),
        rb3=vm(4, HALVES, nb, cb),
        po=vm(4, rows, cb),
        gb=vm(2, NX, NY, rows, cb),
        gx=vm(tok, cb),
        acc=vf(2, rows, wide),
        bs=vm(HALVES, tok, cb),
        br=vm(HALVES, tok, cb),
        es=vm(tok, wide),
        er=vm(tok, wide),
        co=vm(rows, cb),
        bps=vm(2, rows, rank),
        bpr=vm(2, tok, rank),
        hi=vf(2, HALVES, 2 * NT, 8, tok),
        ls=[vm(tok, parts * rank) for parts in (4, 1, 2, 1)],
        ai=[vm(NT, piece, parts * rank) for parts in (4, 1, 2, 1)],
        ao=[vm(rows, parts * rank) for parts in (4, 1, 2, 1)],
        l_sem=dma(23),
        e_sem=[dma(23), dma(23)],
        r_sem=[dma(4, HALVES, 13), dma(4, HALVES, 13)],
        g_sem=[dma(2, HALVES, 13), dma(2, HALVES, 13)],
        a_sem=[dma(4, 3), dma(4, 3)],
        h_sem=[dma(2, HALVES), dma(2, HALVES)],
        p_sem=[dma(3, HALVES), dma(3, HALVES)],
        m_sem=[dma(12), dma(12)],
    )
    return table


def kernel(
    tree,
    sections,
    width,
    base_weight,
    pol_down,
    pol_up,
    old_down,
    old_up,
    pol_in,
    ref_in,
    grad_in,
    stash,
    fresh_pol,
    fresh_ref,
    targets,
    final_gain,
    token_side,
    ref_logratio,
    pol_out,
    ref_out,
    grad_out,
    grad_down,
    grad_up,
    *buffers,
):
    b = SimpleNamespace(**jax.tree.unflatten(tree, buffers))
    wb, xin, pb, gb, acc = b.wb, b.xin, b.pb, b.gb, b.acc
    rows, wide = xin.shape[1:]
    tok, cb = rows // 2, wide // 2
    rank = pol_up.shape[1]
    piece = tok // NT

    s = lax.axis_index("section")
    t = lax.axis_index("tensor")
    c = lax.axis_index("dp")
    x, y = t // NY, t % NY
    ox, oc = 1 - x, 1 - c
    ring = [(y + i) % NY for i in range(NY)]
    order = (ring[2], ring[1], ring[3], ring[0])
    y1, y2, y3 = ring[1:]
    is_last = s == sections - 1
    is_first = s == 0
    pair = (s, t, oc)
    over = (s, ox * NY + y, c)
    ways = ((s, x * NY + y1, c), (s, x * NY + y3, c))
    near = (y1, y3)

    my_rows = pl.ds(pl.multiple_of(c * tok, tok), tok)
    its_rows = pl.ds(pl.multiple_of(oc * tok, tok), tok)
    my_cols = pl.ds(pl.multiple_of(c * cb, cb), cb)
    its_cols = pl.ds(pl.multiple_of(oc * cb, cb), cb)

    def half(h):
        return pl.ds(h * tok, tok)

    def size(part):
        return pl.ds(0, part.size)

    def inner(part, h):
        return pl.ds(part.start - h * tok, part.size)

    def f32(ref, *index):
        return ref[index].astype(F32)

    def send(src, dst, group, index, device):
        return pltpu.make_async_remote_copy(
            src_ref=src,
            dst_ref=dst,
            send_sem=group[0].at[index],
            recv_sem=group[1].at[index],
            device_id=device,
            device_id_type=MESH,
        )

    def weight_cols(xx, yy, core):
        first = pl.multiple_of((xx * NY + yy) * wide + core * cb, cb)
        return base_weight.at[0, :, pl.ds(first, cb)]

    own, away, place = {}, {}, {}
    for j in range(4):
        for side in range(2):
            xx, yy, name = (ox, x)[side], order[j], ("w", j, side)
            own[name] = (weight_cols(xx, yy, c), wb.at[xx, yy, my_cols, :])
            away[name] = (weight_cols(xx, yy, oc), wb.at[xx, yy, my_cols, :])

    def both(name, src, dst):
        own[name] = away[name] = (src, dst)

    def columns(name, src, dst):
        own[name] = (src.at[:, my_cols], dst)
        away[name] = (src.at[:, its_cols], dst)

    both("dn", pol_down.at[0], b.dn.at[my_cols])
    both("do", old_down.at[0], b.do.at[my_cols])
    both("p0", pol_in.at[0], xin.at[0, my_rows])
    both("r0", ref_in.at[0], xin.at[1, my_rows])
    both("fp", fresh_pol.at[0], xin.at[2, my_rows])
    both("fr", fresh_ref.at[0], xin.at[3, my_rows])
    columns("g0", grad_in.at[0], gb.at[0, x, y, my_rows])
    columns("s0", stash.at[0, 0], b.sb.at[0, my_rows])
    columns("s1", stash.at[0, 1], b.sb.at[1, my_rows])
    columns("t0", targets.at[0], b.tg.at[0, my_rows])
    columns("t1", targets.at[1], b.tg.at[1, my_rows])
    own["st"] = (stash.at[0], b.st)
    own["up"] = (pol_up.at[0], b.up)
    own["ou"] = (old_up.at[0], b.ou)
    away["ax"] = (b.ax.at[c], b.ax.at[c])
    for name in list(own) + ["ax"]:
        place[name] = len(place)

    def local(name):
        return pltpu.make_async_copy(*own[name], b.l_sem.at[place[name]])

    def swap(name):
        return send(*away[name], b.e_sem, place[name], pair)

    weights = [("w", j, side) for j in range(4) for side in range(2)]
    for name in ["p0", *weights[:2], "dn", "do", "g0", "up", "ou", "r0", "st", *weights[2:], "s0", "s1", "t0", "t1"]:
        local(name).start()

    @pl.when(is_first)
    def _():
        local("fp").start()
        local("fr").start()

    me = 2 * t + c
    barrier = pltpu.get_barrier_semaphore()

    def greet(d, _):
        other = (me + d) % (2 * NT)
        pl.semaphore_signal(barrier, inc=1, device_id=(s, other // 2, other % 2), device_id_type=MESH)
        return 0

    after = ((s + 1) % sections, t, c)
    before = ((s + sections - 1) % sections, t, c)
    lax.fori_loop(1, 2 * NT, greet, 0)
    pl.semaphore_signal(barrier, inc=1, device_id=after, device_id_type=MESH)
    pl.semaphore_signal(barrier, inc=1, device_id=before, device_id_type=MESH)
    pl.semaphore_wait(barrier, 2 * NT + 1)

    for name in ["p0", *weights[:2], "g0", "dn", "do", *weights[2:4], "r0", *weights[4:]]:
        swap(name).start()

    side = token_side[...]
    signs = (side == 1).astype(F32) - (side == 2).astype(F32)
    ratios = jnp.concatenate([jnp.broadcast_to(ref_logratio[:, k : k + 1], (1, tok)) for k in range(2)], axis=0)
    b.ax[c] = jnp.concatenate([signs, ratios, signs, ratios], axis=0)
    for name in ("ax", "t0", "s0", "s1", "t1"):
        swap(name).start()

    @pl.when(is_first)
    def _():
        swap("fp").start()
        swap("fr").start()

    def schedule(plan, forward_rows, backward_rows, last):
        seen, sent = set(), []

        def need(*wanted):
            for name in wanted:
                if name in seen:
                    continue
                seen.add(name)
                if isinstance(name, tuple) and name[0] == "g":
                    g_copy(*name[1:]).wait_recv()
                    continue
                if name != "ax":
                    local(name).wait()
                if name in away:
                    swap(name).wait_recv()
                    sent.append(swap(name))

        def start(copy):
            copy.start()
            sent.append(copy)

        def part_rows(index):
            return pl.ds(pl.multiple_of(index * piece, piece), piece)

        here = pl.ds(pl.multiple_of(c * tok + t * piece, piece), piece)

        def ars(i):
            ls, ai = b.ls[i], b.ai[i]
            if i == 0:
                need("dn", "do", "p0", "r0", "st", "up", "ou")
                b.dr[...] = mixed(b.dn[...], b.do[...])
                b.ur[...] = mixed(b.up[...], b.ou[...])
                terms = (
                    (xin.at[0, my_rows], b.dn),
                    (xin.at[1, my_rows], b.dr),
                    (b.st.at[0], b.dn),
                    (b.st.at[1], b.dn),
                )
            elif i == 2:
                terms = ((xin.at[2, my_rows], b.dn), (xin.at[3, my_rows], b.dr))
            else:
                k = i // 2
                send(b.bps.at[k, its_rows], b.bpr.at[k], b.m_sem, k, pair).wait_recv()
                ls[...] = (f32(b.bps, k, my_rows) + f32(b.bpr, k)).astype(BF)
                terms = ()
            for q, (ref, down) in enumerate(terms):
                ls[:, q * rank : (q + 1) * rank] = nn(ref[...], down[...]).astype(BF)

            def one(d, _):
                tt = (t + d) % NT
                send(ls.at[part_rows(tt)], ai.at[t], b.a_sem, (i, 0), (s, tt, c)).start()
                return 0

            lax.fori_loop(1, NT, one, 0)
            ai[t] = ls[part_rows(t)]

        def arr(i):
            ai, ao = b.ai[i], b.ao[i]
            seven = ai.at[pl.ds(0, NT - 1)]
            pltpu.make_async_copy(seven, seven, b.a_sem[1].at[i, 0]).wait()
            total = ai[0].astype(F32)
            for d in range(1, NT):
                total += ai[d].astype(F32)
            ao[here] = total.astype(BF)

            def one(d, _):
                tt = (t + d) % NT
                send(ao.at[here], ao.at[here], b.a_sem, (i, 1), (s, tt, c)).start()
                return 0

            lax.fori_loop(1, NT, one, 0)

        def arh(i):
            ao = b.ao[i]
            most = ao.at[pl.ds(0, piece * (NT - 1))]
            pltpu.make_async_copy(most, most, b.a_sem[1].at[i, 1]).wait()
            start(send(ao.at[my_rows], ao.at[my_rows], b.a_sem, (i, 2), pair))

        def ard(i):
            ao = b.ao[i]
            send(ao.at[my_rows], ao.at[my_rows], b.a_sem, (i, 2), pair).wait_recv()

        def sums_sent(i):
            seven = b.ai[i].at[pl.ds(0, NT - 1)]
            pltpu.make_async_copy(seven, seven, b.a_sem[0].at[i, 0]).wait()
            most = b.ao[i].at[pl.ds(0, piece * (NT - 1))]
            pltpu.make_async_copy(most, most, b.a_sem[0].at[i, 1]).wait()

        def a_part(p, h):
            return pl.ds(h * tok, forward_rows[p][h])

        def b_part(p, h):
            return pl.ds(h * tok + forward_rows[p][h], tok - forward_rows[p][h])

        def a_half(p, h, up):
            part = a_part(p, h)
            return split(part.start, part.size, 1)[up]

        def b_half(p, h, up):
            part = b_part(p, h)
            return split(part.start, part.size, 0)[up]

        def c_a1(p, h, j):
            part = a_part(p, h)
            return send(pb.at[p, ox, order[j], part], b.ra1.at[p, h, j, size(part)], b.r_sem, (p, h, j), over)

        def c_a2(p, h, up):
            part = a_half(p, h, up)
            return send(pb.at[p, x, y2, part], b.ra2.at[p, h, up, size(part)], b.r_sem, (p, h, 4 + up), ways[up])

        def c_b1(p, h, up):
            part = b_half(p, h, up)
            return send(pb.at[p, :, y2, part], b.rb1.at[p, h, up, :, size(part)], b.r_sem, (p, h, 6 + up), ways[up])

        def c_b2(p, h, up):
            part = b_part(p, h)
            return send(pb.at[p, :, near[up], part], b.rb2.at[p, h, up, :, size(part)], b.r_sem, (p, h, 8 + up), ways[up])

        def c_b3(p, h):
            part = b_part(p, h)
            return send(pb.at[p, ox, y, part], b.rb3.at[p, h, size(part)], b.r_sem, (p, h, 10), over)

        def c_a3(p, h, up):
            part = a_part(p, h)
            return send(pb.at[p, x, near[up], part], b.ra3.at[p, h, up, size(part)], b.r_sem, (p, h, 11 + up), ways[up])

        def pr(p, _, j):
            if p < 2:
                need(("p0", "r0")[p])
            need(("w", j, 0), ("w", j, 1))
            for xx in (ox, x):
                pb[p, xx, order[j]] = nn(xin[p], wb[xx, order[j]]).astype(BF)

        def a1(p, h, j):
            start(c_a1(p, h, j))

        def b1(p, h):
            start(c_b1(p, h, 0))
            start(c_b1(p, h, 1))

        def b2(p, h, up):
            part, yy = b_half(p, h, up), near[up]
            c_b1(p, h, up).wait_recv()
            for xx in range(NX):
                pb[p, xx, yy, part] = (f32(pb, p, xx, yy, part) + f32(b.rb1, p, h, up, xx, size(part))).astype(BF)
            start(c_b2(p, h, up))

        def a2(p, h):
            part = a_part(p, h)
            c_a1(p, h, 0).wait_recv()
            pb[p, x, y2, part] = (f32(pb, p, x, y2, part) + f32(b.ra1, p, h, 0, size(part))).astype(BF)
            start(c_a2(p, h, 0))
            start(c_a2(p, h, 1))

        def b3(p, h):
            part = b_part(p, h)
            n = size(part)
            c_b2(p, h, 0).wait_recv()
            c_b2(p, h, 1).wait_recv()
            pb[p, ox, y, part] = (
                f32(pb, p, ox, y, part) + f32(b.rb2, p, h, 0, ox, n) + f32(b.rb2, p, h, 1, ox, n)
            ).astype(BF)
            start(c_b3(p, h))

        def a3(p, h, up):
            yy, part, rest = near[up], a_half(p, h, up), a_half(p, h, 1 - up)
            c_a1(p, h, 1 + up).wait_recv()
            c_a2(p, h, up).wait_recv()
            pb[p, x, yy, part] = (
                f32(pb, p, x, yy, part)
                + f32(b.ra1, p, h, 1 + up, inner(part, h))
                + f32(b.ra2, p, h, up, size(part))
            ).astype(BF)
            pb[p, x, yy, rest] = (f32(pb, p, x, yy, rest) + f32(b.ra1, p, h, 1 + up, inner(rest, h))).astype(BF)
            start(c_a3(p, h, up))

        def fin(p, h):
            c_a1(p, h, 3).wait_recv()
            c_a3(p, h, 0).wait_recv()
            c_a3(p, h, 1).wait_recv()
            c_b3(p, h).wait_recv()
            low, up_ref = b.ao[p // 2 * 2], (b.up, b.ur)[p % 2][...]
            low_cols = pl.ds(p % 2 * rank, rank)
            a, bb = a_part(p, h), b_part(p, h)
            na, nb = size(a), size(bb)
            summed = (
                f32(pb, p, x, y, a) + f32(b.ra1, p, h, 3, na) + f32(b.ra3, p, h, 0, na) + f32(b.ra3, p, h, 1, na),
                f32(pb, p, x, y, bb)
                + f32(b.rb2, p, h, 0, x, nb)
                + f32(b.rb2, p, h, 1, x, nb)
                + f32(b.rb3, p, h, nb),
            )
            for part, total in zip((a, bb), summed):
                adapted = ADAPTER_SCALE * nn(low[part, low_cols], up_ref)
                b.po[p, part] = (f32(xin, p, part, my_cols) + total + adapted).astype(BF)
            if p < 2:
                if not last:
                    start(c_pass(p, h))
                return
            out = (pol_out, ref_out)[p - 2]

            @pl.when(c == h)
            def _():
                out[0, :, my_cols] = b.po[p, half(h)]

            @pl.when(c != h)
            def _():
                c_out(p, h).start()

        def c_out(p, h):
            return send(b.po.at[p, half(h)], (pol_out, ref_out)[p - 2].at[0, :, my_cols], b.m_sem, p, pair)

        def c_pass(i, h):
            if i < 2:
                return send(b.po.at[i, half(h)], xin.at[2 + i, half(h), my_cols], b.p_sem, (i, h), after)
            return send(b.co.at[half(h)], gb.at[1, x, y, half(h)], b.p_sem, (2, h), before)

        def c_take(i, h):
            block = xin.at[2 + i, half(h), my_cols]
            return send(block, block, b.m_sem, 4 + 2 * i + h, pair)

        def unless_first(body):
            if last:
                body()
            else:
                pl.when(jnp.logical_not(is_first))(body)

        def tk(i, h):
            @unless_first
            def _():
                c_pass(i, h).wait_recv()
                c_take(i, h).start()

        def td(i, h):
            @unless_first
            def _():
                c_take(i, h).wait()

            if not last and ("fresh", i) not in seen:
                seen.add(("fresh", i))

                @pl.when(is_first)
                def _():
                    local(("fp", "fr")[i]).wait()
                    swap(("fp", "fr")[i]).wait()

        def hs(k, h):
            need(("t0", "t1")[k])
            p, part = 2 * k, half(h)
            gain = final_gain[:, my_cols]
            hidden = f32(b.po, p, part)
            squares = jnp.sum(hidden * hidden, axis=1, keepdims=True)
            inner_sum = jnp.sum(hidden * gain * f32(b.tg, k, part), axis=1, keepdims=True)
            lane = lax.broadcasted_iota(jnp.int32, (tok, 128), 1)
            b.hi[k, h, me] = jnp.where(lane == 0, squares, inner_sum).T[:8]

            def one(d, _):
                other = (me + d) % (2 * NT)
                slot = b.hi.at[k, h, me]
                send(slot, slot, b.h_sem, (k, h), (s, other // 2, other % 2)).start()
                return 0

            lax.fori_loop(1, 2 * NT, one, 0)

        def hw(k, h):
            if k == 0:
                need("g0")
            need("ax")
            others = b.hi.at[k, h, pl.ds(0, 2 * NT - 1)]
            pltpu.make_async_copy(others, others, b.h_sem[1].at[k, h]).wait()
            total = b.hi[k, h, 0]
            for d in range(1, 2 * NT):
                total += b.hi[k, h, d]
            sums = jnp.concatenate([total] * 16, axis=0).T
            squares, dot = sums[:, 0:1], sums[:, 1:2]
            r = lax.rsqrt(squares / width + NORM_EPSILON)
            aux = jnp.concatenate([b.ax[h]] * 16, axis=0).T
            sign, ratio = aux[:, k : k + 1], aux[0:1, 2 + k : 3 + k]
            margin = PREF_BETA * (jnp.sum(dot * r * sign, axis=0, keepdims=True) - ratio)
            weight = -LOSS_SCALE * PREF_BETA * jax.nn.sigmoid(-margin) * sign
            gain = final_gain[:, my_cols]
            hidden, target = f32(b.po, 2 * k, half(h)), f32(b.tg, k, half(h))
            g = weight * (r * gain * target - (dot * r * r * r / width) * hidden)
            gb[k, x, y, half(h)] = g.astype(BF)

        def head_sent(k, h):
            others = b.hi.at[k, h, pl.ds(0, 2 * NT - 1)]
            pltpu.make_async_copy(others, others, b.h_sem[0].at[k, h]).wait()

        routes = ((), (), (), (), (2,), (2,), (0,), (1,), (0,), (1,), (4,), (5,), (6, 7))

        def g_copy(k, h, i):
            n = backward_rows[k][h]
            first = h * tok
            a, bb = pl.ds(first, n), pl.ds(first + n, tok - n)
            low, high = split(first, tok, 0)
            a_low, a_high = split(first, n, 0)
            xx, yy, part, device = (
                (x, y, half(h), ways[0]),
                (x, y, half(h), ways[1]),
                (x, y, a, over),
                (x, y, bb, over),
                (ox, y, a, ways[0]),
                (ox, y, a, ways[1]),
                (x, y3, low, ways[0]),
                (x, y1, high, ways[1]),
                (x, y3, bb, over),
                (x, y1, bb, over),
                (ox, y3, a_low, ways[0]),
                (ox, y1, a_high, ways[1]),
                (x, y2, bb, over),
            )[i]
            block = gb.at[k, xx, yy, part]
            return send(block, block, b.g_sem, (k, h, i), device)

        def g(k, h, i):
            if k == 0 and not last:
                need("g0")
            need(*[("g", k, h, q) for q in routes[i]])
            start(g_copy(k, h, i))

        def th(k, q):
            need(*weights)
            if k == 0 and not last:
                need("g0")
            xx, yy, wanted = (
                (x, y, ()),
                (x, y3, (0,)),
                (x, y1, (1,)),
                (ox, y, (2, 3)),
                (x, y2, (6, 7)),
                (ox, y3, (4, 8)),
                (ox, y1, (5, 9)),
                (ox, y2, (10, 11, 12)),
            )[q]
            need(*[("g", k, h, i) for h in range(HALVES) for i in wanted])
            term = nt(gb[k, xx, yy], wb[xx, yy])
            acc[k] = term if q == 0 else acc[k] + term

        def c_acc(h):
            return send(b.bs.at[h], b.br.at[h], b.m_sem, 8 + h, pair)

        def c_end():
            return send(b.es, b.er, b.m_sem, 10, pair)

        def c_gx():
            return send(gb.at[1, x, y, its_rows], b.gx, b.m_sem, 11, pair)

        def acc_(k, h):
            if k == 0:
                b.bs[h] = acc[0, half(h), its_cols].astype(BF)
                start(c_acc(h))
            else:

                @pl.when(c != h)
                def _():
                    b.es[...] = acc[1, half(h)].astype(BF)
                    c_end().start()

        def bp(k):
            need("up")
            if k == 0 and not last:
                need("g0")
            b.bps[k] = nt(gb[k, x, y], b.up[...]).astype(BF)
            start(send(b.bps.at[k, its_rows], b.bpr.at[k], b.m_sem, k, pair))
            if k == 1:
                start(c_gx())

        def cfin(h):
            c_acc(h).wait_recv()
            back = b.ao[1][half(h)]
            adapted = ADAPTER_SCALE * nt(back, b.dn[my_cols])
            total = f32(gb, 0, x, y, half(h)) + acc[0, half(h), my_cols] + f32(b.br, h)
            b.co[half(h)] = (total + adapted).astype(BF)
            if last:
                start(c_pass(2, h))
            else:

                @pl.when(jnp.logical_not(is_first))
                def _():
                    c_pass(2, h).start()

        def cw(h):
            c_pass(2, h).wait_recv()

        def gr(k):
            need("s0", "s1")
            back = b.ao[2 * k + 1][...]
            if last:
                stored, low = xin[2 * k, :, my_cols], b.ao[2 * k][:, 0:rank]
            else:
                stored, low = b.sb[k], b.ao[0][:, (2 + k) * rank : (3 + k) * rank]
            down = ADAPTER_SCALE * tn(stored, back)
            up = ADAPTER_SCALE * tn(low, gb[k, x, y])
            if k == 0:
                grad_down[0] = down
                grad_up[0] = up
            else:
                grad_down[0] += down
                grad_up[0] += up

        def end():
            c_gx().wait_recv()
            c_end().wait_recv()
            back = b.ao[3][my_rows]
            for cols, cotangent in ((my_cols, gb.at[1, x, y, my_rows]), (its_cols, b.gx)):
                adapted = ADAPTER_SCALE * nt(back, b.dn[cols])
                total = cotangent[...].astype(F32) + acc[1, my_rows, cols] + b.er[:, cols].astype(F32)
                grad_out[0, :, cols] = (total + adapted).astype(BF)
            need(*[name for name in place if name not in ("fp", "fr")])
            for p in (2, 3):
                c_out(p, 0).wait()
            c_end().wait_send()
            for copy in sent:
                copy.wait_send()
            if not last:

                @unless_first
                def _():
                    for h in range(HALVES):
                        c_pass(2, h).wait_send()

            for i in range(4):
                sums_sent(i)
            if last:
                for k in range(2):
                    for h in range(HALVES):
                        head_sent(k, h)

        steps = (
            pr, a1, a2, a3, b1, b2, b3, fin, ars, arr, arh, ard, hs, hw, g, th, bp, acc_, cfin, cw, tk, td, gr, end
        )
        for step, *index in plan:
            steps[step](*index)

    @pl.when(is_last)
    def _():
        schedule(PLAN_LAST, *ROWS_LAST, True)

    @pl.when(jnp.logical_not(is_last))
    def _():
        schedule(PLAN_OTHERS, *ROWS_OTHERS, False)


def put(*refs):
    copies = [pltpu.make_async_copy(refs[i], refs[5 + i], refs[10].at[i]) for i in range(5)]
    for copy in copies:
        copy.start()
    for copy in copies:
        copy.wait()


def on_device(sections, width, *operands):
    pol_in = operands[5]
    tok, wide = pol_in.shape[1:]
    cb = wide // 2
    rank = operands[1].shape[2]
    operands = list(operands)
    operands[12] = operands[12].reshape(1, wide)
    operands[14] = operands[14].reshape(1, 2)
    buffers, tree = jax.tree.flatten(scratch(tok, cb, rank))
    anywhere = pl.BlockSpec(memory_space=pl.ANY)
    inside = pl.BlockSpec(memory_space=pltpu.VMEM)
    in_vmem = (12, 13, 14)
    outs = (
        jax.ShapeDtypeStruct((1, tok, wide), BF),
        jax.ShapeDtypeStruct((1, tok, wide), BF),
        jax.ShapeDtypeStruct((1, tok, wide), BF),
        jax.ShapeDtypeStruct((1, cb, rank), F32),
        jax.ShapeDtypeStruct((1, rank, cb), F32),
    )
    results = pl.pallas_call(
        functools.partial(kernel, tree, sections, width),
        out_shape=outs,
        in_specs=[inside if i in in_vmem else anywhere for i in range(15)],
        out_specs=[inside] * 5,
        scratch_shapes=buffers,
        compiler_params=pltpu.CompilerParams(
            collective_id=0, has_side_effects=True, vmem_limit_bytes=56 * 1024 * 1024
        ),
        name="relay",
    )(*operands)
    return pl.pallas_call(
        put,
        out_shape=outs,
        in_specs=[inside] * 5,
        out_specs=[anywhere] * 5,
        scratch_shapes=[pltpu.SemaphoreType.DMA((5,))],
        name="put",
    )(*results)


def solution(mesh):
    in_specs = (
        P("section", ("tensor", "dp"), None),
        P("section", ("tensor", "dp"), None),
        P("section", None, ("tensor", "dp")),
        P("section", ("tensor", "dp"), None),
        P("section", None, ("tensor", "dp")),
        P("section", "dp", "tensor"),
        P("section", "dp", "tensor"),
        P("section", "dp", "tensor"),
        P("section", None, "dp", "tensor"),
        P(None, "dp", "tensor"),
        P(None, "dp", "tensor"),
        P(None, "dp", "tensor"),
        P("tensor"),
        P(None, "dp"),
        P(None, "dp"),
    )
    out_specs = (
        P("section", "dp", "tensor"),
        P("section", "dp", "tensor"),
        P("section", "dp", "tensor"),
        P("section", ("tensor", "dp"), None),
        P("section", None, ("tensor", "dp")),
    )
    sections = mesh.shape["section"]

    def whole(base_weight, *rest):
        body = functools.partial(on_device, sections, base_weight.shape[1])
        return jax.shard_map(
            body, mesh=mesh, in_specs=in_specs, out_specs=out_specs, check_vma=False
        )(base_weight, *rest)

    return whole
```
